256 devices in a mesh: frames: 32 (over y, x, core), planes: 8 (over z).
Axes of the slice: x: 4, y: 4, z: 8, core: 2. Of those that a mesh axis runs over, the one named last changes fastest.
Arguments:
- recording: float32 [256, 8, 256, 128], P('frames', 'planes'), may hold values from -30 to 30
- template: float32 [8, 256, 128], P('planes'), may hold values from -4 to 4
- shifts: int32 [256, 8, 2], P('frames', 'planes'), may hold values from -16 to 16
- support: int32 [256, 96], replicated, may hold values from 0 to 255, as said below
- temporal_init: float32 [256, 256], replicated, may hold values from 0 to 0.3
- spatial_init: float32 [256, 8, 32768], P(None, 'planes', 'frames'), may hold values from 0 to 29
Outputs:
- temporal: float32 [256, 256], replicated
- spatial: float32 [256, 8, 32768], P(None, 'planes', 'frames')
The draws below stay inside these ranges and needn't reach their ends.
Inputs may be any that keep to these rules, and one draw needn't show every extreme that they name: `support`: each component names 96 different tiles.
All inputs are finite; a program needn't handle non-finite values.
Results may differ from the reference program's by a relative error of at most 0.0001.
Values sent between devices are 32-bit elements; how exact they have to be, the bound alone decides.
No kernel may reach another device: no remote copies, remote signals or barrier semaphores. Data moves between devices by JAX's collectives and lax.ppermute only.
A program may use at most 128 MiB of HBM per device.

```python
import jax
import jax.numpy as jnp
from jax import lax

HEIGHT = 256
WIDTH = 128
COMP = 256
TILE = 1024
NTREND = 16
ITERS = 1
MAXS = 16
PLANES = 8
FRAMES = 256
TILES = 256
NSUP = 96


def shared_parts(key):
    template_key = jax.random.fold_in(key, 11)
    shift_key = jax.random.fold_in(key, 12)
    template = jnp.clip(jax.random.normal(template_key, (PLANES, HEIGHT, WIDTH), jnp.float32), -4.0, 4.0)
    shifts = jax.random.randint(shift_key, (FRAMES, PLANES, 2), -MAXS, MAXS + 1).astype(jnp.int32)
    return (template, shifts)


def bright_pixels(key):
    picks = jax.random.uniform(jax.random.fold_in(key, 16), (PLANES, HEIGHT, WIDTH), jnp.float32, 0.0, 1.0)
    gain = jnp.where(picks < 0.01, 10.0, 1.0)
    return gain.astype(jnp.float32)


def place_template(picture, offsets):
    return jnp.roll(picture, (-offsets[0], -offsets[1]), axis=(0, 1))


def draw_template(key, part):
    template, shifts = shared_parts(key)
    return template


def draw_shifts(key, part):
    template, shifts = shared_parts(key)
    return shifts


def draw_recording(key, part):
    template, shifts = shared_parts(key)
    data_gain = 1.0 + 0.25 * (bright_pixels(key) - 1.0)
    amplitude = jax.random.uniform(jax.random.fold_in(key, 13), (FRAMES,), jnp.float32, 0.2, 1.5)
    levels = jnp.arange(PLANES).astype(jnp.float32) / max(PLANES - 1, 1)
    brightness = jnp.power(3.0, levels)
    noise_key = jax.random.fold_in(key, 14)
    noise = jnp.clip(jax.random.normal(noise_key, (FRAMES, PLANES, HEIGHT, WIDTH), jnp.float32), -4.0, 4.0)
    placed = jax.vmap(lambda offsets: jax.vmap(place_template)(template, offsets))(shifts)
    placed_gain = jax.vmap(lambda offsets: jax.vmap(place_template)(data_gain, offsets))(shifts)
    movie = brightness[None, :, None, None] * placed_gain * (amplitude[:, None, None, None] * placed + noise)
    return jnp.clip(movie, -30.0, 30.0).astype(jnp.float32)


def draw_spatial_init(key, part):
    gain = bright_pixels(key).reshape(PLANES, HEIGHT * WIDTH)
    factor_key = jax.random.fold_in(key, 17)
    comp_level = jnp.exp(jax.random.uniform(jax.random.fold_in(factor_key, 1), (COMP,), jnp.float32, jnp.log(0.3), jnp.log(3.0)))
    tile_level = jax.random.uniform(jax.random.fold_in(factor_key, 2), (COMP, PLANES, HEIGHT * WIDTH // TILE), jnp.float32, 0.5, 1.5)
    tile_level = jnp.repeat(tile_level, TILE, axis=2)
    pixel_level = jnp.exp(jax.random.uniform(jax.random.fold_in(factor_key, 3), (PLANES, HEIGHT * WIDTH), jnp.float32, 0.0, jnp.log(4.0)))
    base_key = jax.random.fold_in(factor_key, 4)
    base = jax.random.uniform(base_key, (COMP, PLANES, HEIGHT * WIDTH), jnp.float32, 0.0, 0.1)
    values = base * comp_level[:, None, None] * tile_level * (pixel_level * gain)[None]
    return values.astype(jnp.float32)


def pick_tiles(component_key):
    scores = jax.random.randint(component_key, (TILES,), 0, 1 << 20) * TILES + jnp.arange(TILES)
    values, indices = jax.lax.top_k(scores, NSUP)
    return indices.astype(jnp.int32)


def draw_support(key, part):
    component_keys = jax.random.split(jax.random.fold_in(key, 15), COMP)
    return jax.vmap(pick_tiles)(component_keys)


def setup_inputs(seed: int = 0) -> dict:
    streams_of = jax.random.split(jax.random.key(seed), 7)
    return {
        "recording": draw_recording(jax.random.fold_in(streams_of[6], 71), 0),
        "template": draw_template(jax.random.fold_in(streams_of[6], 71), 0),
        "shifts": draw_shifts(jax.random.fold_in(streams_of[6], 71), 0),
        "support": draw_support(jax.random.fold_in(streams_of[6], 71), 0),
        "temporal_init": jnp.clip(jax.random.uniform(streams_of[4], (FRAMES, COMP), jnp.float32, 0.0, 0.3), 0.0, 0.3),
        "spatial_init": draw_spatial_init(jax.random.fold_in(streams_of[6], 71), 0),
    }


epsilon = 1e-06

def matmul(left_side, right_side):
    return jnp.dot(left_side, right_side, precision=lax.Precision.HIGHEST, preferred_element_type=jnp.float32)

def cosine_table(frame_count, basis_order):
    times = jnp.arange(frame_count).astype(jnp.float32)
    orders = jnp.arange(basis_order).astype(jnp.float32)
    scales = jnp.where(orders == 0, jnp.sqrt(1.0 / frame_count), jnp.sqrt(2.0 / frame_count)).astype(jnp.float32)
    return (jnp.cos(jnp.pi * (times[:, None] + 0.5) * orders[None, :] / frame_count) * scales[None, :]).astype(jnp.float32)

def shift_frame(picture, offsets):
    return jnp.roll(picture, (offsets[0], offsets[1]), axis=(0, 1))

def reference(recording, template, shifts, support, temporal_init, spatial_init):
    registered = jax.vmap(jax.vmap(shift_frame))(recording, shifts)
    numerator = lax.optimization_barrier(jnp.sum(registered * template[None], axis=(1, 2, 3)))
    energy = lax.optimization_barrier(jnp.sum(registered * registered, axis=(1, 2, 3)))
    template_energy = jnp.sum(template * template)
    weight = numerator / jnp.sqrt(energy * template_energy + epsilon)
    series = (registered * weight[:, None, None, None]).reshape(FRAMES, PLANES * HEIGHT * WIDTH)
    cosine_basis = cosine_table(FRAMES, NTREND)
    detrended = series - matmul(cosine_basis, matmul(cosine_basis.T, series))
    tile_ids = jnp.arange(TILES).astype(jnp.int32)
    covered = jnp.any(support[:, :, None] == tile_ids[None, None, :], axis=1).astype(jnp.float32)
    support_mask = jnp.repeat(covered, TILE, axis=1)
    spatial = spatial_init.reshape(COMP, PLANES * HEIGHT * WIDTH) * support_mask
    temporal = temporal_init
    for iteration in range(ITERS):
        spatial_gram = matmul(spatial, spatial.T)
        cross = matmul(detrended, spatial.T)
        temporal_grad = matmul(temporal, spatial_gram) - cross
        grad_square = jnp.sum(temporal_grad * temporal_grad)
        grad_curve = jnp.sum(temporal_grad * matmul(temporal_grad, spatial_gram))
        temporal = jnp.maximum(temporal - grad_square / (grad_curve + epsilon) * temporal_grad, 0.0)
        temporal_gram = matmul(temporal.T, temporal)
        spatial_grad = (matmul(temporal_gram, spatial) - matmul(temporal.T, detrended)) * support_mask
        grad_square = jnp.sum(spatial_grad * spatial_grad)
        grad_curve = jnp.sum(spatial_grad * matmul(temporal_gram, spatial_grad))
        spatial = jnp.maximum(spatial - grad_square / (grad_curve + epsilon) * spatial_grad, 0.0)
    return (temporal, spatial.reshape(COMP, PLANES, HEIGHT * WIDTH))
```

```python
import numpy as np
import jax
import jax.numpy as jnp
from jax import lax
from jax.experimental import pallas as pl
from jax.experimental.pallas import tpu as pltpu
from jax.sharding import PartitionSpec as P

HEIGHT = 256
WIDTH = 128
COMP = 256
FRAMES = 256
PLANES = 8
TILE = 1024
NTREND = 16
GROUP = 32
LOCAL = 8
ROWS = TILE // WIDTH
PACK = 640
epsilon = 1e-06

VMEM = pl.BlockSpec(memory_space=pltpu.VMEM)
SMEM = pl.BlockSpec(memory_space=pltpu.SMEM)
PARAMS = pltpu.CompilerParams(vmem_limit_bytes=48 * 1024 * 1024)


def f32(*shape):
    return jax.ShapeDtypeStruct(shape, jnp.float32)


def dot(left, right, dims=((1,), (0,))):
    return lax.dot_general(
        left, right, (dims, ((), ())),
        precision=lax.Precision.HIGHEST, preferred_element_type=jnp.float32,
    )


def cosine_table():
    times = np.arange(FRAMES)[:, None] + 0.5
    orders = np.arange(NTREND)[None, :]
    scales = np.where(orders == 0, np.sqrt(1.0 / FRAMES), np.sqrt(2.0 / FRAMES))
    return (np.cos(np.pi * times * orders / FRAMES) * scales).astype(np.float32)


def register_kernel(shift_ref, movie_ref, out_ref):
    frame = pl.program_id(0)
    down = jnp.mod(shift_ref[0, frame], HEIGHT)
    right = jnp.mod(shift_ref[1, frame], WIDTH)
    picture = pltpu.roll(movie_ref[0], right, 1)
    picture = pltpu.roll(picture, down, 0)
    out_ref[:, 0] = picture.reshape(GROUP, ROWS, WIDTH)


def mask_row(place_ref, support_ref):
    tile = place_ref[1] * GROUP + place_ref[0]
    hits = jnp.where(support_ref[...] == tile, 1.0, 0.0)
    return jnp.max(hits, axis=0, keepdims=True)


def mask_columns(row):
    return jnp.transpose(jnp.broadcast_to(row, (128, COMP)))


def gram_kernel(place_ref, series_ref, spatial_ref, support_ref, template_ref, pack_ref, stack_ref):
    mask = mask_columns(mask_row(place_ref, support_ref))
    start = pl.multiple_of(place_ref[0] * ROWS, ROWS)
    picture = template_ref[pl.ds(start, ROWS), :]
    numerator = jnp.zeros((FRAMES, WIDTH), jnp.float32)
    energy = jnp.zeros((FRAMES, WIDTH), jnp.float32)
    for row in range(ROWS):
        columns = slice(row * WIDTH, (row + 1) * WIDTH)
        series = series_ref[pl.ds(row, FRAMES, stride=ROWS), :]
        spatial = spatial_ref[pl.ds(row, COMP, stride=ROWS), :] * mask
        stack_ref[:COMP, columns] = spatial
        stack_ref[COMP:, columns] = series
        numerator += series * picture[row:row + 1]
        energy += series * series
    products = dot(stack_ref[...], stack_ref[:COMP, :], ((1,), (1,)))
    pack_ref[:, :COMP] = products[:COMP]
    pack_ref[:, COMP:2 * COMP] = products[COMP:]
    lane = lax.broadcasted_iota(jnp.int32, (FRAMES, 128), 1)
    extra = jnp.where(lane == 2, jnp.sum(picture * picture), 0.0)
    extra = jnp.where(lane == 1, jnp.sum(energy, axis=1, keepdims=True), extra)
    extra = jnp.where(lane == 0, jnp.sum(numerator, axis=1, keepdims=True), extra)
    pack_ref[:, 2 * COMP:] = extra


def spread_kernel(in_ref, out_ref):
    total = jnp.sum(in_ref[...], axis=0)
    out_ref[...] = jnp.broadcast_to(total[None], out_ref.shape)


def step_kernel(place_ref, pack_ref, temporal_ref, basis_ref, support_ref, stack_ref,
                out_ref, grad_ref, sums_ref):
    gram = pack_ref[:, :COMP]
    basis = basis_ref[...]

    def detrend(values):
        return values - dot(basis, dot(basis, values, ((0,), (0,))))

    energy = pack_ref[:, 2 * COMP + 1:2 * COMP + 2] * pack_ref[:, 2 * COMP + 2:2 * COMP + 3]
    weight = pack_ref[:, 2 * COMP:2 * COMP + 1] / jnp.sqrt(energy + epsilon)
    cross = detrend(pack_ref[:, COMP:2 * COMP] * weight)
    temporal = temporal_ref[...]
    grad = dot(temporal, gram) - cross
    step = jnp.sum(grad * grad) / (jnp.sum(grad * dot(grad, gram)) + epsilon)
    temporal = jnp.maximum(temporal - step * grad, 0.0)
    out_ref[...] = temporal
    temporal_gram = dot(temporal, temporal, ((0,), (0,)))
    projector = detrend(temporal) * weight
    mask = mask_columns(mask_row(place_ref, support_ref))[:, :1]
    spatial_grad = (
        dot(temporal_gram, stack_ref[:COMP, :]) - dot(projector, stack_ref[COMP:, :], ((0,), (0,)))
    ) * mask
    grad_ref[...] = spatial_grad
    square = jnp.sum(spatial_grad * spatial_grad)
    curve = jnp.sum(spatial_grad * dot(temporal_gram, spatial_grad))
    lane = lax.broadcasted_iota(jnp.int32, sums_ref.shape, 2)
    sums_ref[...] = jnp.where(lane == 0, square, jnp.where(lane == 1, curve, 0.0))


def final_kernel(sums_ref, stack_ref, grad_ref, out_ref):
    totals = jnp.sum(jnp.sum(sums_ref[...], axis=0), axis=0, keepdims=True)
    lane = lax.broadcasted_iota(jnp.int32, totals.shape, 1)
    square = jnp.sum(jnp.where(lane == 0, totals, 0.0))
    curve = jnp.sum(jnp.where(lane == 1, totals, 0.0))
    step = square / (curve + epsilon)
    for row in range(ROWS):
        columns = slice(row * WIDTH, (row + 1) * WIDTH)
        out_ref[pl.ds(row, COMP, stride=ROWS), :] = jnp.maximum(
            stack_ref[:, columns] - step * grad_ref[:, columns], 0.0
        )


def exchange(values, axes):
    return lax.all_to_all(values, axes, split_axis=0, concat_axis=0, tiled=True)


def body(recording, template, shifts, support, temporal_init, spatial_init):
    movie = recording.reshape(LOCAL, HEIGHT, WIDTH)
    shift_table = shifts.transpose(1, 2, 0).reshape(2, LOCAL)
    support_table = support.T
    place = jnp.stack([lax.axis_index("frames"), lax.axis_index("planes")]).astype(jnp.int32)
    payload = pl.pallas_call(
        register_kernel,
        out_shape=f32(GROUP, LOCAL, ROWS, WIDTH),
        grid=(LOCAL,),
        in_specs=[SMEM, pl.BlockSpec((1, HEIGHT, WIDTH), lambda f: (f, 0, 0))],
        out_specs=pl.BlockSpec((GROUP, 1, ROWS, WIDTH), lambda f: (0, f, 0, 0)),
        compiler_params=PARAMS,
        name="register",
    )(shift_table, movie)
    series = exchange(payload, "frames").reshape(FRAMES * ROWS, WIDTH)
    spatial = spatial_init.reshape(COMP * ROWS, WIDTH)
    pack, stack = pl.pallas_call(
        gram_kernel,
        out_shape=(f32(FRAMES, PACK), f32(COMP + FRAMES, TILE)),
        in_specs=[SMEM, VMEM, VMEM, VMEM, VMEM],
        out_specs=(VMEM, VMEM),
        compiler_params=PARAMS,
        name="grams",
    )(place, series, spatial, support_table, template.reshape(HEIGHT, WIDTH))

    def spread(values, copies):
        return pl.pallas_call(
            spread_kernel,
            out_shape=f32(copies, *values.shape[1:]),
            in_specs=[VMEM],
            out_specs=VMEM,
            compiler_params=PARAMS,
            name="spread",
        )(values)

    part = exchange(pack.reshape(GROUP, LOCAL, PACK), "frames")
    part = exchange(spread(part, PLANES), "planes")
    pack = exchange(spread(part, GROUP), "frames").reshape(FRAMES, PACK)
    temporal, grad, sums = pl.pallas_call(
        step_kernel,
        out_shape=(f32(FRAMES, COMP), f32(COMP, TILE), f32(GROUP * PLANES, 1, 128)),
        in_specs=[SMEM] + [VMEM] * 5,
        out_specs=(VMEM, VMEM, VMEM),
        compiler_params=PARAMS,
        name="steps",
    )(place, pack, temporal_init, jnp.asarray(cosine_table()), support_table, stack)
    sums = exchange(sums, ("frames", "planes")).reshape(GROUP, PLANES, 128)
    spatial = pl.pallas_call(
        final_kernel,
        out_shape=f32(COMP * ROWS, WIDTH),
        grid=(1,),
        in_specs=[
            pl.BlockSpec((GROUP, PLANES, 128), lambda i: (0, 0, 0)),
            pl.BlockSpec((COMP, TILE), lambda i: (0, 0)),
            pl.BlockSpec((COMP, TILE), lambda i: (0, 0)),
        ],
        out_specs=pl.BlockSpec((COMP * ROWS, WIDTH), lambda i: (0, 0)),
        compiler_params=PARAMS,
        name="update",
    )(sums, stack, grad)
    return (temporal, spatial.reshape(COMP, 1, TILE))


def solution(mesh):
    placed = (
        P("frames", "planes", None, None),
        P("planes", None, None),
        P("frames", "planes", None),
        P(),
        P(),
        P(None, "planes", "frames"),
    )
    return jax.shard_map(
        body,
        mesh=mesh,
        in_specs=placed,
        out_specs=(P(), P(None, "planes", "frames")),
        check_vma=False,
    )
```

```python
import numpy as np
import jax
import jax.numpy as jnp
from jax import lax
from jax.experimental import pallas as pl
from jax.experimental.pallas import tpu as pltpu
from jax.sharding import PartitionSpec as P

HEIGHT = 256
WIDTH = 128
COMP = 256
FRAMES = 256
PLANES = 8
TILE = 1024
NTREND = 16
GROUP = 32
LOCAL = 8
ROWS = TILE // WIDTH
PACK = 512
HALF = 128
MAXS = 16
epsilon = 1e-06

VMEM = pl.BlockSpec(memory_space=pltpu.VMEM)
SMEM = pl.BlockSpec(memory_space=pltpu.SMEM)
HBM = pl.BlockSpec(memory_space=pltpu.HBM)
MIB = 1024 * 1024
NN = ((1,), (0,))
NT = ((1,), (1,))


def f32(*shape):
    return jax.ShapeDtypeStruct(shape, jnp.float32)


def b16(*shape):
    return jax.ShapeDtypeStruct(shape, jnp.bfloat16)


def split(values):
    high = values.astype(jnp.bfloat16)
    return high, (values - high.astype(jnp.float32)).astype(jnp.bfloat16)


def dot(left, right, dims=NN):
    def product(a, b):
        return lax.dot_general(a, b, (dims, ((), ())), preferred_element_type=jnp.float32)

    return product(left[0], right[0]) + (product(left[0], right[1]) + product(left[1], right[0]))


def trend_projector():
    times = np.arange(FRAMES)[:, None] + 0.5
    orders = np.arange(NTREND)[None, :]
    scales = np.where(orders == 0, np.sqrt(1.0 / FRAMES), np.sqrt(2.0 / FRAMES))
    basis = np.cos(np.pi * times * orders / FRAMES) * scales
    return (basis @ basis.T).astype(np.float32)


def register_kernel(shift_hbm, movie_hbm, out_ref, shift_ref, movie_ref, wide_ref, shift_sem, movie_sem):
    table = pltpu.make_async_copy(shift_hbm, shift_ref, shift_sem)
    table.start()
    copies = [
        pltpu.make_async_copy(movie_hbm.at[frame], movie_ref.at[frame], movie_sem.at[frame])
        for frame in range(LOCAL)
    ]
    for copy in copies:
        copy.start()
    table.wait()
    for frame in range(LOCAL):
        copies[frame].wait()
        right = jnp.mod(shift_ref[1, frame], WIDTH)
        picture = pltpu.roll(movie_ref[frame], right, 1)
        wide = wide_ref.at[frame]
        wide[pl.ds(0, MAXS), :] = picture[HEIGHT - MAXS:]
        wide[pl.ds(MAXS, HEIGHT), :] = picture
        wide[pl.ds(MAXS + HEIGHT, MAXS), :] = picture[:MAXS]
        moved = wide[pl.ds(MAXS - shift_ref[0, frame], HEIGHT), :]
        out_ref[:, frame] = moved.reshape(GROUP, ROWS, WIDTH)


def spatial_kernel(place_ref, spatial_ref, support_ref, template_ref,
                   stack_ref, high_ref, low_ref, mask_ref, pack_ref, picture_ref):
    start = pl.multiple_of(place_ref[0] * ROWS, ROWS)
    picture_ref[...] = template_ref[pl.ds(start, ROWS), :]
    tile = place_ref[1] * GROUP + place_ref[0]
    hits = jnp.where(support_ref[...] == tile, 1.0, 0.0)
    covered = jnp.max(hits, axis=0, keepdims=True)
    mask = jnp.transpose(jnp.broadcast_to(covered, (128, COMP)))
    mask_ref[...] = mask
    for row in range(ROWS):
        columns = slice(row * WIDTH, (row + 1) * WIDTH)
        spatial = spatial_ref[pl.ds(row, COMP, stride=ROWS), :] * mask
        stack_ref[:, columns] = spatial
        high_ref[:, columns], low_ref[:, columns] = split(spatial)
    parts = (high_ref[...], low_ref[...])
    gram = dot(parts, parts, NT)
    pack_ref[:HALF, :] = gram[:HALF, :]
    pack_ref[HALF:, :HALF] = gram[HALF:, HALF:]
    pack_ref[HALF:, HALF:] = pltpu.roll(gram[:HALF, HALF:], HALF // 2, 1)


def cross_kernel(series_ref, picture_ref, spatial_high_ref, spatial_low_ref, gram_ref,
                 pack_ref, high_ref, low_ref):
    picture = picture_ref[...]
    numerator = jnp.zeros((FRAMES, WIDTH), jnp.float32)
    energy = jnp.zeros((FRAMES, WIDTH), jnp.float32)
    for row in range(ROWS):
        columns = slice(row * WIDTH, (row + 1) * WIDTH)
        series = series_ref[pl.ds(row, FRAMES, stride=ROWS), :]
        high_ref[:, columns], low_ref[:, columns] = split(series)
        numerator += series * picture[row:row + 1]
        energy += series * series
    lane = lax.broadcasted_iota(jnp.int32, (FRAMES, 128), 1)
    extra = jnp.where(lane == HALF // 2, jnp.sum(numerator, axis=1, keepdims=True), jnp.sum(picture * picture))
    extra = jnp.where(lane == HALF // 2 + 1, jnp.sum(energy, axis=1, keepdims=True), extra)
    pack_ref[:, :HALF] = gram_ref[:, :HALF]
    pack_ref[:, HALF:2 * HALF] = jnp.where(lane < HALF // 2, gram_ref[:, HALF:], extra)
    pack_ref[:, COMP:] = dot(
        (high_ref[...], low_ref[...]), (spatial_high_ref[...], spatial_low_ref[...]), NT
    )


def spread_kernel(in_ref, out_ref):
    total = jnp.sum(in_ref[...], axis=0)
    out_ref[...] = jnp.broadcast_to(total[None], out_ref.shape)


def step_kernel(pack_ref, temporal_ref, trend_ref, mask_ref, spatial_high_ref, spatial_low_ref,
                high_ref, low_ref, out_ref, grad_ref, sums_ref):
    lane = lax.broadcasted_iota(jnp.int32, (HALF, HALF), 1)
    corner = jnp.where(
        lane < HALF // 2,
        pack_ref[:HALF, HALF:2 * HALF],
        pltpu.roll(pack_ref[HALF:, HALF:2 * HALF], HALF // 2, 1),
    )
    gram = split(jnp.concatenate([
        jnp.concatenate([pack_ref[:HALF, :HALF], corner], axis=1),
        jnp.concatenate([jnp.transpose(corner), pack_ref[HALF:, :HALF]], axis=1),
    ], axis=0))
    extra = pack_ref[:, HALF:2 * HALF]
    first = HALF // 2
    energy = extra[:, first + 1:first + 2] * extra[:, first + 2:first + 3]
    weight = extra[:, first:first + 1] / jnp.sqrt(energy + epsilon)
    trend = split(trend_ref[...])
    cross = pack_ref[:, COMP:] * weight
    cross = cross - dot(trend, split(cross))
    temporal = temporal_ref[...]
    grad = dot(split(temporal), gram) - cross
    step = jnp.sum(grad * grad) / (jnp.sum(grad * dot(split(grad), gram)) + epsilon)
    temporal = jnp.maximum(temporal - step * grad, 0.0)
    out_ref[...] = temporal
    flipped = jnp.transpose(temporal)
    parts = split(flipped)
    temporal_gram = split(dot(parts, parts, NT))
    weight_row = jnp.transpose(jnp.broadcast_to(weight, (FRAMES, 128)))[:1]
    projector = split((flipped - dot(parts, trend)) * weight_row)
    spatial_grad = (
        dot(temporal_gram, (spatial_high_ref[...], spatial_low_ref[...]))
        - dot(projector, (high_ref[...], low_ref[...]))
    ) * mask_ref[:, :1]
    grad_ref[...] = spatial_grad
    square = jnp.sum(spatial_grad * spatial_grad)
    curve = jnp.sum(spatial_grad * dot(temporal_gram, split(spatial_grad)))
    lane = lax.broadcasted_iota(jnp.int32, sums_ref.shape, 2)
    sums_ref[...] = jnp.where(lane == 0, square, jnp.where(lane == 1, curve, 0.0))


BLOCKS = 4


def final_kernel(sums_ref, stack_ref, grad_ref, out_ref):
    totals = jnp.sum(jnp.sum(sums_ref[...], axis=0), axis=0, keepdims=True)
    lane = lax.broadcasted_iota(jnp.int32, totals.shape, 1)
    square = jnp.sum(jnp.where(lane == 0, totals, 0.0))
    curve = jnp.sum(jnp.where(lane == 1, totals, 0.0))
    step = square / (curve + epsilon)
    size = COMP // BLOCKS
    rows = pl.ds(pl.multiple_of(pl.program_id(0) * size, size), size)
    for row in range(ROWS):
        columns = pl.ds(row * WIDTH, WIDTH)
        out_ref[pl.ds(row, size, stride=ROWS), :] = jnp.maximum(
            stack_ref[rows, columns] - step * grad_ref[rows, columns], 0.0
        )


def exchange(values, axes):
    return lax.all_to_all(values, axes, split_axis=0, concat_axis=0, tiled=True)


def call(kernel, name, out_shape, in_specs, cost=None, vmem=24, **options):
    single = not isinstance(out_shape, tuple)
    options.setdefault("out_specs", VMEM if single else (VMEM,) * len(out_shape))
    return pl.pallas_call(
        kernel, out_shape=out_shape, in_specs=in_specs, name=name, cost_estimate=cost,
        compiler_params=pltpu.CompilerParams(vmem_limit_bytes=vmem * MIB), **options,
    )


def body(recording, template, shifts, support, temporal_init, spatial_init):
    movie = recording.reshape(LOCAL, HEIGHT, WIDTH)
    shift_table = shifts.transpose(1, 2, 0).reshape(2, LOCAL)
    place = jnp.stack([lax.axis_index("frames"), lax.axis_index("planes")]).astype(jnp.int32)
    payload = call(
        register_kernel, "register", f32(GROUP, LOCAL, ROWS, WIDTH), [HBM, HBM], vmem=60,
        scratch_shapes=[
            pltpu.SMEM((2, LOCAL), jnp.int32),
            pltpu.VMEM((LOCAL, HEIGHT, WIDTH), jnp.float32),
            pltpu.VMEM((LOCAL, HEIGHT + 2 * MAXS, WIDTH), jnp.float32),
            pltpu.SemaphoreType.DMA,
            pltpu.SemaphoreType.DMA((LOCAL,)),
        ],
    )(shift_table, movie)
    series = exchange(payload, "frames").reshape(FRAMES * ROWS, WIDTH)
    spatial = spatial_init.reshape(COMP * ROWS, WIDTH)
    stack, spatial_high, spatial_low, mask, gram, picture = call(
        spatial_kernel, "spatial",
        (f32(COMP, TILE), b16(COMP, TILE), b16(COMP, TILE), f32(COMP, 128), f32(COMP, COMP),
         f32(ROWS, WIDTH)),
        [SMEM] + [VMEM] * 3,
        cost=pl.CostEstimate(flops=6 * COMP * COMP * TILE, bytes_accessed=4 << 20, transcendentals=0),
    )(place, spatial, support.T, template.reshape(HEIGHT, WIDTH))
    pack, high, low = call(
        cross_kernel, "cross", (f32(FRAMES, PACK), b16(FRAMES, TILE), b16(FRAMES, TILE)),
        [VMEM] * 5,
    )(series, picture, spatial_high, spatial_low, gram)

    def spread(values, copies):
        return call(spread_kernel, "spread", f32(copies, *values.shape[1:]), [VMEM])(values)

    part = exchange(pack.reshape(GROUP, LOCAL, PACK), "frames")
    part = exchange(spread(part, PLANES), "planes")
    pack = exchange(spread(part, GROUP), "frames").reshape(FRAMES, PACK)
    temporal, grad, sums = call(
        step_kernel, "steps",
        (f32(FRAMES, COMP), f32(COMP, TILE), f32(GROUP * PLANES, 1, 128)),
        [VMEM] * 8,
    )(pack, temporal_init, jnp.asarray(trend_projector()), mask, spatial_high, spatial_low, high, low)
    sums = exchange(sums, ("frames", "planes")).reshape(GROUP, PLANES, 128)
    spatial = call(
        final_kernel, "update", f32(COMP * ROWS, WIDTH), [VMEM] * 3,
        grid=(BLOCKS,),
        out_specs=pl.BlockSpec((COMP * ROWS // BLOCKS, WIDTH), lambda i: (i, 0)),
    )(sums, stack, grad)
    return (temporal, spatial.reshape(COMP, 1, TILE))


def solution(mesh):
    placed = (
        P("frames", "planes", None, None),
        P("planes", None, None),
        P("frames", "planes", None),
        P(),
        P(),
        P(None, "planes", "frames"),
    )
    return jax.shard_map(
        body,
        mesh=mesh,
        in_specs=placed,
        out_specs=(P(), P(None, "planes", "frames")),
        check_vma=False,
    )
```

```python
import numpy as np
import jax
import jax.numpy as jnp
from jax import lax
from jax.experimental import pallas as pl
from jax.experimental.pallas import tpu as pltpu
from jax.sharding import PartitionSpec as P

HEIGHT = 256
WIDTH = 128
COMP = 256
FRAMES = 256
PLANES = 8
TILE = 1024
NTREND = 16
GROUP = 32
LOCAL = 8
ROWS = TILE // WIDTH
PACK = 512
HALF = 128
MAXS = 16
epsilon = 1e-06

VMEM = pl.BlockSpec(memory_space=pltpu.VMEM)
SMEM = pl.BlockSpec(memory_space=pltpu.SMEM)
HBM = pl.BlockSpec(memory_space=pltpu.HBM)
MIB = 1024 * 1024
NN = ((1,), (0,))
NT = ((1,), (1,))


def f32(*shape):
    return jax.ShapeDtypeStruct(shape, jnp.float32)


def b16(*shape):
    return jax.ShapeDtypeStruct(shape, jnp.bfloat16)


def split(values):
    high = values.astype(jnp.bfloat16)
    return high, (values - high.astype(jnp.float32)).astype(jnp.bfloat16)


def dot(left, right, dims=NN):
    def product(a, b):
        return lax.dot_general(a, b, (dims, ((), ())), preferred_element_type=jnp.float32)

    return product(left[0], right[0]) + (product(left[0], right[1]) + product(left[1], right[0]))


def trend_projector():
    times = np.arange(FRAMES)[:, None] + 0.5
    orders = np.arange(NTREND)[None, :]
    scales = np.where(orders == 0, np.sqrt(1.0 / FRAMES), np.sqrt(2.0 / FRAMES))
    basis = np.cos(np.pi * times * orders / FRAMES) * scales
    return (basis @ basis.T).astype(np.float32)


def register_kernel(shift_hbm, movie_hbm, out_hbm, shift_ref, movie_ref, wide_ref, moved_ref,
                    shift_sem, movie_sem, moved_sem):
    table = pltpu.make_async_copy(shift_hbm, shift_ref, shift_sem)
    table.start()
    copies = [
        pltpu.make_async_copy(movie_hbm.at[frame], movie_ref.at[frame], movie_sem.at[frame])
        for frame in range(LOCAL)
    ]
    for copy in copies:
        copy.start()
    table.wait()
    stores = []
    for frame in range(LOCAL):
        copies[frame].wait()
        right = jnp.mod(shift_ref[1, frame], WIDTH)
        picture = pltpu.roll(movie_ref[frame], right, 1)
        wide = wide_ref.at[frame]
        wide[pl.ds(0, MAXS), :] = picture[HEIGHT - MAXS:]
        wide[pl.ds(MAXS, HEIGHT), :] = picture
        wide[pl.ds(MAXS + HEIGHT, MAXS), :] = picture[:MAXS]
        moved = wide[pl.ds(MAXS - shift_ref[0, frame], HEIGHT), :]
        moved_ref[frame] = moved.reshape(GROUP, ROWS, WIDTH)
        stores.append(
            pltpu.make_async_copy(moved_ref.at[frame], out_hbm.at[:, frame], moved_sem.at[frame])
        )
        stores[frame].start()
    for store in stores:
        store.wait()


def spatial_kernel(place_ref, spatial_ref, support_ref, template_ref,
                   stack_ref, high_ref, low_ref, mask_ref, pack_ref, picture_ref):
    start = pl.multiple_of(place_ref[0] * ROWS, ROWS)
    picture_ref[...] = template_ref[pl.ds(start, ROWS), :]
    tile = place_ref[1] * GROUP + place_ref[0]
    hits = jnp.where(support_ref[...] == tile, 1.0, 0.0)
    covered = jnp.max(hits, axis=0, keepdims=True)
    mask = jnp.transpose(jnp.broadcast_to(covered, (128, COMP)))
    mask_ref[...] = mask
    for row in range(ROWS):
        columns = slice(row * WIDTH, (row + 1) * WIDTH)
        spatial = spatial_ref[pl.ds(row, COMP, stride=ROWS), :] * mask
        stack_ref[pl.ds(row, COMP, stride=ROWS), :] = spatial
        high_ref[:, columns], low_ref[:, columns] = split(spatial)
    parts = (high_ref[...], low_ref[...])
    gram = dot(parts, parts, NT)
    pack_ref[:HALF, :] = gram[:HALF, :]
    pack_ref[HALF:, :HALF] = gram[HALF:, HALF:]
    pack_ref[HALF:, HALF:] = pltpu.roll(gram[:HALF, HALF:], HALF // 2, 1)


def cross_kernel(core_ref, series_ref, picture_ref, spatial_high_ref, spatial_low_ref, gram_ref,
                 keep_ref, give_ref, high_ref, low_ref, pack_ref):
    picture = picture_ref[...]
    numerator = jnp.zeros((FRAMES, WIDTH), jnp.float32)
    energy = jnp.zeros((FRAMES, WIDTH), jnp.float32)
    for row in range(ROWS):
        columns = slice(row * WIDTH, (row + 1) * WIDTH)
        series = series_ref[pl.ds(row, FRAMES, stride=ROWS), :]
        high_ref[:, columns], low_ref[:, columns] = split(series)
        numerator += series * picture[row:row + 1]
        energy += series * series
    lane = lax.broadcasted_iota(jnp.int32, (FRAMES, 128), 1)
    extra = jnp.where(lane == HALF // 2, jnp.sum(numerator, axis=1, keepdims=True), jnp.sum(picture * picture))
    extra = jnp.where(lane == HALF // 2 + 1, jnp.sum(energy, axis=1, keepdims=True), extra)
    pack_ref[:, :HALF] = gram_ref[:, :HALF]
    pack_ref[:, HALF:2 * HALF] = jnp.where(lane < HALF // 2, gram_ref[:, HALF:], extra)
    pack_ref[:, COMP:] = dot(
        (high_ref[...], low_ref[...]), (spatial_high_ref[...], spatial_low_ref[...]), NT
    )
    mine = pl.multiple_of(core_ref[2] * HALF, HALF)
    other = pl.multiple_of(HALF - core_ref[2] * HALF, HALF)
    keep_ref[...] = pack_ref[pl.ds(mine, HALF), :]
    give_ref[...] = pack_ref[pl.ds(other, HALF), :]


def add_kernel(left_ref, right_ref, out_ref):
    out_ref[...] = left_ref[...] + right_ref[...]


def spread_kernel(in_ref, out_ref):
    total = jnp.sum(in_ref[...], axis=0)
    out_ref[...] = jnp.broadcast_to(total[None], out_ref.shape)


def step_kernel(core_ref, mine_ref, other_ref, temporal_ref, trend_ref, mask_ref,
                spatial_high_ref, spatial_low_ref, high_ref, low_ref,
                out_ref, grad_ref, sums_ref, pack_ref):
    mine = pl.multiple_of(core_ref[2] * HALF, HALF)
    other = pl.multiple_of(HALF - core_ref[2] * HALF, HALF)
    pack_ref[pl.ds(mine, HALF), :] = mine_ref[...]
    pack_ref[pl.ds(other, HALF), :] = other_ref[...]
    lane = lax.broadcasted_iota(jnp.int32, (HALF, HALF), 1)
    corner = jnp.where(
        lane < HALF // 2,
        pack_ref[:HALF, HALF:2 * HALF],
        pltpu.roll(pack_ref[HALF:, HALF:2 * HALF], HALF // 2, 1),
    )
    gram = split(jnp.concatenate([
        jnp.concatenate([pack_ref[:HALF, :HALF], corner], axis=1),
        jnp.concatenate([jnp.transpose(corner), pack_ref[HALF:, :HALF]], axis=1),
    ], axis=0))
    extra = pack_ref[:, HALF:2 * HALF]
    first = HALF // 2
    energy = extra[:, first + 1:first + 2] * extra[:, first + 2:first + 3]
    weight = extra[:, first:first + 1] / jnp.sqrt(energy + epsilon)
    trend = split(trend_ref[...])
    cross = pack_ref[:, COMP:] * weight
    cross = cross - dot(trend, split(cross))
    temporal = temporal_ref[...]
    grad = dot(split(temporal), gram) - cross
    step = jnp.sum(grad * grad) / (jnp.sum(grad * dot(split(grad), gram)) + epsilon)
    temporal = jnp.maximum(temporal - step * grad, 0.0)
    out_ref[...] = temporal
    flipped = jnp.transpose(temporal)
    parts = split(flipped)
    temporal_gram = split(dot(parts, parts, NT))
    weight_row = jnp.transpose(jnp.broadcast_to(weight, (FRAMES, 128)))[:1]
    projector = split((flipped - dot(parts, trend)) * weight_row)
    spatial_grad = (
        dot(temporal_gram, (spatial_high_ref[...], spatial_low_ref[...]))
        - dot(projector, (high_ref[...], low_ref[...]))
    ) * mask_ref[:, :1]
    for row in range(ROWS):
        grad_ref[pl.ds(row, COMP, stride=ROWS), :] = spatial_grad[:, row * WIDTH:(row + 1) * WIDTH]
    square = jnp.sum(spatial_grad * spatial_grad)
    curve = jnp.sum(spatial_grad * dot(temporal_gram, split(spatial_grad)))
    lane = lax.broadcasted_iota(jnp.int32, sums_ref.shape, 2)
    sums_ref[...] = jnp.where(lane == 0, square, jnp.where(lane == 1, curve, 0.0))


BLOCKS = 4


def final_kernel(sums_ref, stack_ref, grad_ref, out_hbm, out_ref, sems):
    totals = jnp.sum(jnp.sum(sums_ref[...], axis=0), axis=0, keepdims=True)
    lane = lax.broadcasted_iota(jnp.int32, totals.shape, 1)
    square = jnp.sum(jnp.where(lane == 0, totals, 0.0))
    curve = jnp.sum(jnp.where(lane == 1, totals, 0.0))
    step = square / (curve + epsilon)
    size = COMP * ROWS // BLOCKS
    stores = []
    for block in range(BLOCKS):
        rows = pl.ds(block * size, size)
        out_ref[rows, :] = jnp.maximum(stack_ref[rows, :] - step * grad_ref[rows, :], 0.0)
        stores.append(pltpu.make_async_copy(out_ref.at[rows], out_hbm.at[rows], sems.at[block]))
        stores[block].start()
    for store in stores:
        store.wait()


def exchange(values, axes, groups=None):
    return lax.all_to_all(
        values, axes, split_axis=0, concat_axis=0, axis_index_groups=groups, tiled=True
    )


def swap(values):
    return lax.ppermute(values, "frames", [(index, index ^ 1) for index in range(GROUP)])


def call(kernel, name, out_shape, in_specs, cost=None, vmem=24, **options):
    single = not isinstance(out_shape, tuple)
    options.setdefault("out_specs", VMEM if single else (VMEM,) * len(out_shape))
    return pl.pallas_call(
        kernel, out_shape=out_shape, in_specs=in_specs, name=name, cost_estimate=cost,
        compiler_params=pltpu.CompilerParams(vmem_limit_bytes=vmem * MIB), **options,
    )


def body(recording, template, shifts, support, temporal_init, spatial_init):
    movie = recording.reshape(LOCAL, HEIGHT, WIDTH)
    shift_table = shifts.transpose(1, 2, 0).reshape(2, LOCAL)
    index = lax.axis_index("frames")
    place = jnp.stack([index, lax.axis_index("planes"), index & 1]).astype(jnp.int32)
    payload = call(
        register_kernel, "register", f32(GROUP, LOCAL, ROWS, WIDTH), [HBM, HBM], vmem=60, out_specs=HBM,
        scratch_shapes=[
            pltpu.SMEM((2, LOCAL), jnp.int32),
            pltpu.VMEM((LOCAL, HEIGHT, WIDTH), jnp.float32),
            pltpu.VMEM((LOCAL, HEIGHT + 2 * MAXS, WIDTH), jnp.float32),
            pltpu.VMEM((LOCAL, GROUP, ROWS, WIDTH), jnp.float32),
            pltpu.SemaphoreType.DMA,
            pltpu.SemaphoreType.DMA((LOCAL,)),
            pltpu.SemaphoreType.DMA((LOCAL,)),
        ],
    )(shift_table, movie)
    series = exchange(payload, "frames").reshape(FRAMES * ROWS, WIDTH)
    spatial = spatial_init.reshape(COMP * ROWS, WIDTH)
    stack, spatial_high, spatial_low, mask, gram, picture = call(
        spatial_kernel, "spatial",
        (f32(COMP * ROWS, WIDTH), b16(COMP, TILE), b16(COMP, TILE), f32(COMP, 128), f32(COMP, COMP),
         f32(ROWS, WIDTH)),
        [SMEM] + [VMEM] * 3,
        cost=pl.CostEstimate(flops=6 * COMP * COMP * TILE, bytes_accessed=4 << 20, transcendentals=0),
    )(place, spatial, support.T, template.reshape(HEIGHT, WIDTH))
    keep, give, high, low = call(
        cross_kernel, "cross",
        (f32(HALF, PACK), f32(HALF, PACK), b16(FRAMES, TILE), b16(FRAMES, TILE)),
        [SMEM] + [VMEM] * 5,
        scratch_shapes=[pltpu.VMEM((FRAMES, PACK), jnp.float32)],
    )(place, series, picture, spatial_high, spatial_low, gram)

    def spread(values, copies):
        return call(spread_kernel, "spread", f32(copies, *values.shape[1:]), [VMEM])(values)

    chips = [list(range(core, GROUP, 2)) for core in range(2)]
    part = call(add_kernel, "pair", f32(HALF, PACK), [VMEM] * 2)(keep, swap(give))
    part = exchange(part.reshape(GROUP // 2, LOCAL, PACK), "frames", chips)
    part = exchange(spread(part, PLANES), "planes")
    mine = exchange(spread(part, GROUP // 2), "frames", chips).reshape(HALF, PACK)
    temporal, grad, sums = call(
        step_kernel, "steps",
        (f32(FRAMES, COMP), f32(COMP * ROWS, WIDTH), f32(GROUP * PLANES, 1, 128)),
        [SMEM] + [VMEM] * 9,
        scratch_shapes=[pltpu.VMEM((FRAMES, PACK), jnp.float32)],
    )(place, mine, swap(mine), temporal_init, jnp.asarray(trend_projector()), mask,
      spatial_high, spatial_low, high, low)
    sums = exchange(sums, ("frames", "planes")).reshape(GROUP, PLANES, 128)
    spatial = call(
        final_kernel, "update", f32(COMP * ROWS, WIDTH), [VMEM] * 3, out_specs=HBM,
        scratch_shapes=[
            pltpu.VMEM((COMP * ROWS, WIDTH), jnp.float32), pltpu.SemaphoreType.DMA((BLOCKS,)),
        ],
    )(sums, stack, grad)
    return (temporal, spatial.reshape(COMP, 1, TILE))


def solution(mesh):
    placed = (
        P("frames", "planes", None, None),
        P("planes", None, None),
        P("frames", "planes", None),
        P(),
        P(),
        P(None, "planes", "frames"),
    )
    return jax.shard_map(
        body,
        mesh=mesh,
        in_specs=placed,
        out_specs=(P(), P(None, "planes", "frames")),
        check_vma=False,
    )
```

```python
import numpy as np
import jax
import jax.numpy as jnp
from jax import lax
from jax.experimental import pallas as pl
from jax.experimental.pallas import tpu as pltpu
from jax.sharding import PartitionSpec as P

HEIGHT = 256
WIDTH = 128
COMP = 256
FRAMES = 256
PLANES = 8
TILE = 1024
NTREND = 16
GROUP = 32
LOCAL = 8
ROWS = TILE // WIDTH
PACK = 512
HALF = 128
MAXS = 16
epsilon = 1e-06

VMEM = pl.BlockSpec(memory_space=pltpu.VMEM)
SMEM = pl.BlockSpec(memory_space=pltpu.SMEM)
HBM = pl.BlockSpec(memory_space=pltpu.HBM)
MIB = 1024 * 1024
NN = ((1,), (0,))
NT = ((1,), (1,))


def f32(*shape):
    return jax.ShapeDtypeStruct(shape, jnp.float32)


def b16(*shape):
    return jax.ShapeDtypeStruct(shape, jnp.bfloat16)


def split(values):
    high = values.astype(jnp.bfloat16)
    return high, (values - high.astype(jnp.float32)).astype(jnp.bfloat16)


def dot(left, right, dims=NN):
    lefts = jnp.concatenate([left[0], left[0], left[1]], axis=1)
    rights = jnp.concatenate([right[0], right[1], right[0]], axis=dims[1][0])
    return lax.dot_general(lefts, rights, (dims, ((), ())), preferred_element_type=jnp.float32)


def trend_projector():
    times = np.arange(FRAMES)[:, None] + 0.5
    orders = np.arange(NTREND)[None, :]
    scales = np.where(orders == 0, np.sqrt(1.0 / FRAMES), np.sqrt(2.0 / FRAMES))
    basis = np.cos(np.pi * times * orders / FRAMES) * scales
    return (basis @ basis.T).astype(np.float32)


def register_kernel(shift_hbm, movie_hbm, out_hbm, shift_ref, movie_ref, wide_ref, moved_ref,
                    shift_sem, movie_sem, moved_sem):
    table = pltpu.make_async_copy(shift_hbm, shift_ref, shift_sem)
    table.start()
    copies = [
        pltpu.make_async_copy(movie_hbm.at[frame], movie_ref.at[frame], movie_sem.at[frame])
        for frame in range(LOCAL)
    ]
    for copy in copies:
        copy.start()
    table.wait()
    stores = []
    for frame in range(LOCAL):
        copies[frame].wait()
        right = jnp.mod(shift_ref[1, frame], WIDTH)
        picture = pltpu.roll(movie_ref[frame], right, 1)
        wide = wide_ref.at[frame]
        wide[pl.ds(0, MAXS), :] = picture[HEIGHT - MAXS:]
        wide[pl.ds(MAXS, HEIGHT), :] = picture
        wide[pl.ds(MAXS + HEIGHT, MAXS), :] = picture[:MAXS]
        moved = wide[pl.ds(MAXS - shift_ref[0, frame], HEIGHT), :]
        moved_ref[frame] = moved.reshape(GROUP, ROWS, WIDTH)
        stores.append(
            pltpu.make_async_copy(moved_ref.at[frame], out_hbm.at[:, frame], moved_sem.at[frame])
        )
        stores[frame].start()
    for store in stores:
        store.wait()


def spatial_kernel(place_ref, spatial_ref, support_ref, template_ref,
                   stack_ref, high_ref, low_ref, mask_ref, pack_ref, picture_ref, upper_ref):
    upper_ref[...] = jnp.broadcast_to(jnp.where(place_ref[2] == 0, 1.0, 0.0), upper_ref.shape)
    start = pl.multiple_of(place_ref[0] * ROWS, ROWS)
    picture_ref[...] = template_ref[pl.ds(start, ROWS), :]
    tile = place_ref[1] * GROUP + place_ref[0]
    hits = jnp.where(support_ref[...] == tile, 1.0, 0.0)
    covered = jnp.max(hits, axis=0, keepdims=True)
    mask = jnp.transpose(jnp.broadcast_to(covered, (128, COMP)))
    mask_ref[...] = mask
    for row in range(ROWS):
        columns = slice(row * WIDTH, (row + 1) * WIDTH)
        spatial = spatial_ref[pl.ds(row, COMP, stride=ROWS), :] * mask
        stack_ref[pl.ds(row, COMP, stride=ROWS), :] = spatial
        high_ref[:, columns], low_ref[:, columns] = split(spatial)
    parts = (high_ref[...], low_ref[...])
    gram = dot(parts, parts, NT)
    pack_ref[:HALF, :] = gram[:HALF, :]
    pack_ref[HALF:, :HALF] = gram[HALF:, HALF:]
    pack_ref[HALF:, HALF:] = pltpu.roll(gram[:HALF, HALF:], HALF // 2, 1)


def cross_kernel(upper_ref, series_ref, picture_ref, spatial_high_ref, spatial_low_ref, gram_ref,
                 keep_ref, give_ref, high_ref, low_ref):
    picture = picture_ref[...]
    numerator = jnp.zeros((FRAMES, WIDTH), jnp.float32)
    energy = jnp.zeros((FRAMES, WIDTH), jnp.float32)
    for row in range(ROWS):
        columns = slice(row * WIDTH, (row + 1) * WIDTH)
        series = series_ref[pl.ds(row, FRAMES, stride=ROWS), :]
        high_ref[:, columns], low_ref[:, columns] = split(series)
        numerator += series * picture[row:row + 1]
        energy += series * series
    lane = lax.broadcasted_iota(jnp.int32, (FRAMES, 128), 1)
    extra = jnp.where(lane == HALF // 2, jnp.sum(numerator, axis=1, keepdims=True), jnp.sum(picture * picture))
    extra = jnp.where(lane == HALF // 2 + 1, jnp.sum(energy, axis=1, keepdims=True), extra)
    extra = jnp.where(lane < HALF // 2, gram_ref[:, HALF:], extra)
    cross = dot((high_ref[...], low_ref[...]), (spatial_high_ref[...], spatial_low_ref[...]), NT)
    upper = upper_ref[:1, :1] > 0.0
    for columns, values in (
        (slice(0, HALF), gram_ref[:, :HALF]), (slice(HALF, COMP), extra), (slice(COMP, PACK), cross)
    ):
        give_ref[:, columns] = jnp.where(upper, values[HALF:], values[:HALF])
        keep_ref[:, columns] = jnp.where(upper, values[:HALF], values[HALF:])


def add_kernel(left_ref, right_ref, out_ref):
    out_ref[...] = left_ref[...] + right_ref[...]


def spread_kernel(in_ref, out_ref):
    total = jnp.sum(in_ref[...], axis=0)
    out_ref[...] = jnp.broadcast_to(total[None], out_ref.shape)


def step_kernel(upper_ref, mine_ref, other_ref, temporal_ref, trend_ref, mask_ref,
                spatial_high_ref, spatial_low_ref, high_ref, low_ref,
                out_ref, grad_ref, sums_ref):
    first = upper_ref[:1, :1] > 0.0
    upper = jnp.where(first, mine_ref[...], other_ref[...])
    lower = jnp.where(first, other_ref[...], mine_ref[...])
    lane = lax.broadcasted_iota(jnp.int32, (HALF, HALF), 1)
    corner = jnp.where(
        lane < HALF // 2, upper[:, HALF:2 * HALF], pltpu.roll(lower[:, HALF:2 * HALF], HALF // 2, 1)
    )
    gram = split(jnp.concatenate([
        jnp.concatenate([upper[:, :HALF], corner], axis=1),
        jnp.concatenate([jnp.transpose(corner), lower[:, :HALF]], axis=1),
    ], axis=0))
    pack = jnp.concatenate([upper, lower], axis=0)
    extra = pack[:, HALF:2 * HALF]
    first = HALF // 2
    energy = extra[:, first + 1:first + 2] * extra[:, first + 2:first + 3]
    weight = extra[:, first:first + 1] / jnp.sqrt(energy + epsilon)
    trend = split(trend_ref[...])
    cross = pack[:, COMP:] * weight
    cross = cross - dot(trend, split(cross))
    temporal = temporal_ref[...]
    grad = dot(split(temporal), gram) - cross
    step = jnp.sum(grad * grad) / (jnp.sum(grad * dot(split(grad), gram)) + epsilon)
    temporal = jnp.maximum(temporal - step * grad, 0.0)
    out_ref[...] = temporal
    flipped = jnp.transpose(temporal)
    parts = split(flipped)
    temporal_gram = split(dot(parts, parts, NT))
    weight_row = jnp.transpose(jnp.broadcast_to(weight, (FRAMES, 128)))[:1]
    projector = split((flipped - dot(parts, trend)) * weight_row)
    spatial_grad = (
        dot(temporal_gram, (spatial_high_ref[...], spatial_low_ref[...]))
        - dot(projector, (high_ref[...], low_ref[...]))
    ) * mask_ref[:, :1]
    for row in range(ROWS):
        grad_ref[pl.ds(row, COMP, stride=ROWS), :] = spatial_grad[:, row * WIDTH:(row + 1) * WIDTH]
    square = jnp.sum(spatial_grad * spatial_grad)
    curve = jnp.sum(spatial_grad * dot(temporal_gram, split(spatial_grad)))
    lane = lax.broadcasted_iota(jnp.int32, sums_ref.shape, 2)
    sums_ref[...] = jnp.where(lane == 0, square, jnp.where(lane == 1, curve, 0.0))


BLOCKS = 4


def final_kernel(sums_ref, stack_ref, grad_ref, out_hbm, out_ref, sems):
    totals = jnp.sum(jnp.sum(sums_ref[...], axis=0), axis=0, keepdims=True)
    lane = lax.broadcasted_iota(jnp.int32, totals.shape, 1)
    square = jnp.sum(jnp.where(lane == 0, totals, 0.0))
    curve = jnp.sum(jnp.where(lane == 1, totals, 0.0))
    step = square / (curve + epsilon)
    size = COMP * ROWS // BLOCKS
    stores = []
    for block in range(BLOCKS):
        rows = pl.ds(block * size, size)
        out_ref[rows, :] = jnp.maximum(stack_ref[rows, :] - step * grad_ref[rows, :], 0.0)
        stores.append(pltpu.make_async_copy(out_ref.at[rows], out_hbm.at[rows], sems.at[block]))
        stores[block].start()
    for store in stores:
        store.wait()


def exchange(values, axes, groups=None):
    return lax.all_to_all(
        values, axes, split_axis=0, concat_axis=0, axis_index_groups=groups, tiled=True
    )


def swap(values):
    return lax.ppermute(values, "frames", [(index, index ^ 1) for index in range(GROUP)])


def call(kernel, name, out_shape, in_specs, cost=None, vmem=24, **options):
    single = not isinstance(out_shape, tuple)
    options.setdefault("out_specs", VMEM if single else (VMEM,) * len(out_shape))
    return pl.pallas_call(
        kernel, out_shape=out_shape, in_specs=in_specs, name=name, cost_estimate=cost,
        compiler_params=pltpu.CompilerParams(vmem_limit_bytes=vmem * MIB), **options,
    )


def body(recording, template, shifts, support, temporal_init, spatial_init):
    movie = recording.reshape(LOCAL, HEIGHT, WIDTH)
    shift_table = shifts.transpose(1, 2, 0).reshape(2, LOCAL)
    index = lax.axis_index("frames")
    place = jnp.stack([index, lax.axis_index("planes"), index & 1]).astype(jnp.int32)
    payload = call(
        register_kernel, "register", f32(GROUP, LOCAL, ROWS, WIDTH), [HBM, HBM], vmem=60, out_specs=HBM,
        scratch_shapes=[
            pltpu.SMEM((2, LOCAL), jnp.int32),
            pltpu.VMEM((LOCAL, HEIGHT, WIDTH), jnp.float32),
            pltpu.VMEM((LOCAL, HEIGHT + 2 * MAXS, WIDTH), jnp.float32),
            pltpu.VMEM((LOCAL, GROUP, ROWS, WIDTH), jnp.float32),
            pltpu.SemaphoreType.DMA,
            pltpu.SemaphoreType.DMA((LOCAL,)),
            pltpu.SemaphoreType.DMA((LOCAL,)),
        ],
    )(shift_table, movie)
    series = exchange(payload, "frames").reshape(FRAMES * ROWS, WIDTH)
    spatial = spatial_init.reshape(COMP * ROWS, WIDTH)
    stack, spatial_high, spatial_low, mask, gram, picture, upper = call(
        spatial_kernel, "spatial",
        (f32(COMP * ROWS, WIDTH), b16(COMP, TILE), b16(COMP, TILE), f32(COMP, 128), f32(COMP, COMP),
         f32(ROWS, WIDTH), f32(8, 128)),
        [SMEM] + [VMEM] * 3,
        cost=pl.CostEstimate(flops=6 * COMP * COMP * TILE, bytes_accessed=4 << 20, transcendentals=0),
    )(place, spatial, support.T, template.reshape(HEIGHT, WIDTH))
    keep, give, high, low = call(
        cross_kernel, "cross",
        (f32(HALF, PACK), f32(HALF, PACK), b16(FRAMES, TILE), b16(FRAMES, TILE)),
        [VMEM] * 6,
    )(upper, series, picture, spatial_high, spatial_low, gram)

    def spread(values, copies):
        return call(spread_kernel, "spread", f32(copies, *values.shape[1:]), [VMEM])(values)

    chips = [list(range(core, GROUP, 2)) for core in range(2)]
    part = call(add_kernel, "pair", f32(HALF, PACK), [VMEM] * 2)(keep, swap(give))
    part = exchange(part.reshape(GROUP // 2, LOCAL, PACK), "frames", chips)
    part = exchange(spread(part, PLANES), "planes")
    mine = exchange(spread(part, GROUP // 2), "frames", chips).reshape(HALF, PACK)
    temporal, grad, sums = call(
        step_kernel, "steps",
        (f32(FRAMES, COMP), f32(COMP * ROWS, WIDTH), f32(GROUP * PLANES, 1, 128)),
        [VMEM] * 10,
    )(upper, mine, swap(mine), temporal_init, jnp.asarray(trend_projector()), mask,
      spatial_high, spatial_low, high, low)
    sums = exchange(sums, ("frames", "planes")).reshape(GROUP, PLANES, 128)
    spatial = call(
        final_kernel, "update", f32(COMP * ROWS, WIDTH), [VMEM] * 3, out_specs=HBM,
        scratch_shapes=[
            pltpu.VMEM((COMP * ROWS, WIDTH), jnp.float32), pltpu.SemaphoreType.DMA((BLOCKS,)),
        ],
    )(sums, stack, grad)
    return (temporal, spatial.reshape(COMP, 1, TILE))


def solution(mesh):
    placed = (
        P("frames", "planes", None, None),
        P("planes", None, None),
        P("frames", "planes", None),
        P(),
        P(),
        P(None, "planes", "frames"),
    )
    return jax.shard_map(
        body,
        mesh=mesh,
        in_specs=placed,
        out_specs=(P(), P(None, "planes", "frames")),
        check_vma=False,
    )
```

```python
import numpy as np
import jax
import jax.numpy as jnp
from jax import lax
from jax.experimental import pallas as pl
from jax.experimental.pallas import tpu as pltpu
from jax.sharding import PartitionSpec as P

HEIGHT = 256
WIDTH = 128
COMP = 256
FRAMES = 256
PLANES = 8
TILE = 1024
NTREND = 16
GROUP = 32
LOCAL = 8
ROWS = TILE // WIDTH
PACK = 512
HALF = 128
MAXS = 16
BATCH = 4
BLOCKS = 8
epsilon = 1e-06

VMEM = pl.BlockSpec(memory_space=pltpu.VMEM)
SMEM = pl.BlockSpec(memory_space=pltpu.SMEM)
HBM = pl.BlockSpec(memory_space=pltpu.HBM)
MIB = 1024 * 1024
NN = ((1,), (0,))
NT = ((1,), (1,))


def f32(*shape):
    return jax.ShapeDtypeStruct(shape, jnp.float32)


def b16(*shape):
    return jax.ShapeDtypeStruct(shape, jnp.bfloat16)


def split(values):
    high = values.astype(jnp.bfloat16)
    return high, (values - high.astype(jnp.float32)).astype(jnp.bfloat16)


def dot(left, right, dims=NN):
    lefts = jnp.concatenate([left[0], left[0], left[1]], axis=1)
    rights = jnp.concatenate([right[0], right[1], right[0]], axis=dims[1][0])
    return lax.dot_general(lefts, rights, (dims, ((), ())), preferred_element_type=jnp.float32)


def trend_projector():
    times = np.arange(FRAMES)[:, None] + 0.5
    orders = np.arange(NTREND)[None, :]
    scales = np.where(orders == 0, np.sqrt(1.0 / FRAMES), np.sqrt(2.0 / FRAMES))
    basis = np.cos(np.pi * times * orders / FRAMES) * scales
    return (basis @ basis.T).astype(np.float32)


def register_kernel(shift_hbm, movie_hbm, out_hbm, shift_ref, movie_ref, wide_ref, moved_ref,
                    shift_sem, movie_sem, moved_sem):
    table = pltpu.make_async_copy(shift_hbm, shift_ref, shift_sem)
    table.start()
    copies = [
        pltpu.make_async_copy(movie_hbm.at[frame], movie_ref.at[frame], movie_sem.at[frame])
        for frame in range(LOCAL)
    ]
    for copy in copies:
        copy.start()
    table.wait()
    stores = []
    for start in range(0, LOCAL, BATCH):
        frames = range(start, start + BATCH)
        for frame in frames:
            copies[frame].wait()
        for frame in frames:
            picture = pltpu.roll(movie_ref[frame], jnp.mod(shift_ref[1, frame], WIDTH), 1)
            wide = wide_ref.at[frame]
            wide[pl.ds(0, MAXS), :] = picture[HEIGHT - MAXS:]
            wide[pl.ds(MAXS, HEIGHT), :] = picture
            wide[pl.ds(MAXS + HEIGHT, MAXS), :] = picture[:MAXS]
        for frame in frames:
            moved = wide_ref[frame, pl.ds(MAXS - shift_ref[0, frame], HEIGHT), :]
            moved_ref[frame] = moved.reshape(GROUP, ROWS, WIDTH)
        for frame in frames:
            store = pltpu.make_async_copy(moved_ref.at[frame], out_hbm.at[:, frame], moved_sem.at[frame])
            store.start()
            stores.append(store)
    for store in stores:
        store.wait()


def spatial_kernel(place_ref, spatial_ref, support_ref, template_ref,
                   stack_ref, high_ref, low_ref, mask_ref, pack_ref, picture_ref, upper_ref):
    upper_ref[...] = jnp.broadcast_to(jnp.where(place_ref[2] == 0, 1.0, 0.0), upper_ref.shape)
    start = pl.multiple_of(place_ref[0] * ROWS, ROWS)
    picture_ref[...] = template_ref[pl.ds(start, ROWS), :]
    tile = place_ref[1] * GROUP + place_ref[0]
    hits = jnp.where(support_ref[...] == tile, 1.0, 0.0)
    covered = jnp.max(hits, axis=0, keepdims=True)
    mask = jnp.transpose(jnp.broadcast_to(covered, (128, COMP)))
    mask_ref[...] = mask
    for row in range(ROWS):
        columns = slice(row * WIDTH, (row + 1) * WIDTH)
        spatial = spatial_ref[pl.ds(row, COMP, stride=ROWS), :] * mask
        stack_ref[pl.ds(row, COMP, stride=ROWS), :] = spatial
        high_ref[:, columns], low_ref[:, columns] = split(spatial)
    parts = (high_ref[...], low_ref[...])
    gram = dot(parts, parts, NT)
    pack_ref[:HALF, :] = gram[:HALF, :]
    pack_ref[HALF:, :HALF] = gram[HALF:, HALF:]
    pack_ref[HALF:, HALF:] = pltpu.roll(gram[:HALF, HALF:], HALF // 2, 1)


def cross_kernel(upper_ref, series_ref, picture_ref, spatial_high_ref, spatial_low_ref, gram_ref,
                 keep_ref, give_ref, high_ref, low_ref):
    picture = picture_ref[...]
    numerator = jnp.zeros((FRAMES, WIDTH), jnp.float32)
    energy = jnp.zeros((FRAMES, WIDTH), jnp.float32)
    for row in range(ROWS):
        columns = slice(row * WIDTH, (row + 1) * WIDTH)
        series = series_ref[pl.ds(row, FRAMES, stride=ROWS), :]
        high_ref[:, columns], low_ref[:, columns] = split(series)
        numerator += series * picture[row:row + 1]
        energy += series * series
    lane = lax.broadcasted_iota(jnp.int32, (FRAMES, 128), 1)
    extra = jnp.where(lane == HALF // 2, jnp.sum(numerator, axis=1, keepdims=True), jnp.sum(picture * picture))
    extra = jnp.where(lane == HALF // 2 + 1, jnp.sum(energy, axis=1, keepdims=True), extra)
    extra = jnp.where(lane < HALF // 2, gram_ref[:, HALF:], extra)
    cross = dot((high_ref[...], low_ref[...]), (spatial_high_ref[...], spatial_low_ref[...]), NT)
    upper = upper_ref[:1, :1] > 0.0
    for columns, values in (
        (slice(0, HALF), gram_ref[:, :HALF]), (slice(HALF, COMP), extra), (slice(COMP, PACK), cross)
    ):
        give_ref[:, columns] = jnp.where(upper, values[HALF:], values[:HALF])
        keep_ref[:, columns] = jnp.where(upper, values[:HALF], values[HALF:])


def add_kernel(left_ref, right_ref, out_ref):
    out_ref[...] = left_ref[...] + right_ref[...]


def spread_kernel(in_ref, out_ref):
    total = jnp.sum(in_ref[...], axis=0)
    out_ref[...] = jnp.broadcast_to(total[None], out_ref.shape)


def weigh_kernel(in_ref, out_ref):
    total = jnp.sum(in_ref[...], axis=0)
    first = HALF + HALF // 2
    energy = total[:, first + 1:first + 2] * total[:, first + 2:first + 3]
    weight = total[:, first:first + 1] / jnp.sqrt(energy + epsilon)
    column = lax.broadcasted_iota(jnp.int32, (LOCAL, PACK), 1)
    total = jnp.where(column >= COMP, total * weight, jnp.where(column == first, weight, total))
    out_ref[...] = jnp.broadcast_to(total[None], out_ref.shape)


def step_kernel(upper_ref, mine_ref, other_ref, temporal_ref, trend_ref, mask_ref,
                spatial_high_ref, spatial_low_ref, high_ref, low_ref,
                out_ref, grad_ref, sums_ref):
    first = upper_ref[:1, :1] > 0.0
    upper = jnp.where(first, mine_ref[...], other_ref[...])
    lower = jnp.where(first, other_ref[...], mine_ref[...])
    lane = lax.broadcasted_iota(jnp.int32, (HALF, HALF), 1)
    corner = jnp.where(
        lane < HALF // 2, upper[:, HALF:2 * HALF], pltpu.roll(lower[:, HALF:2 * HALF], HALF // 2, 1)
    )
    gram = split(jnp.concatenate([
        jnp.concatenate([upper[:, :HALF], corner], axis=1),
        jnp.concatenate([jnp.transpose(corner), lower[:, :HALF]], axis=1),
    ], axis=0))
    pack = jnp.concatenate([upper, lower], axis=0)
    weight = pack[:, HALF + HALF // 2:HALF + HALF // 2 + 1]
    cross = pack[:, COMP:]
    trend = split(trend_ref[...])
    temporal = temporal_ref[...]
    grad = dot(split(temporal), gram) + dot(trend, split(cross)) - cross
    step = jnp.sum(grad * grad) / (jnp.sum(grad * dot(split(grad), gram)) + epsilon)
    temporal = jnp.maximum(temporal - step * grad, 0.0)
    out_ref[...] = temporal
    flipped = jnp.transpose(temporal)
    parts = split(flipped)
    temporal_gram = split(dot(parts, parts, NT))
    weight_row = jnp.transpose(jnp.broadcast_to(weight, (FRAMES, 128)))[:1]
    projector = split((flipped - dot(parts, trend)) * weight_row)
    spatial_grad = (
        dot(temporal_gram, (spatial_high_ref[...], spatial_low_ref[...]))
        - dot(projector, (high_ref[...], low_ref[...]))
    ) * mask_ref[:, :1]
    for row in range(ROWS):
        grad_ref[pl.ds(row, COMP, stride=ROWS), :] = spatial_grad[:, row * WIDTH:(row + 1) * WIDTH]
    square = jnp.sum(spatial_grad * spatial_grad)
    curve = jnp.sum(spatial_grad * dot(temporal_gram, split(spatial_grad)))
    lane = lax.broadcasted_iota(jnp.int32, sums_ref.shape, 2)
    sums_ref[...] = jnp.where(lane == 0, square, jnp.where(lane == 1, curve, 0.0))


def final_kernel(sums_ref, stack_ref, grad_ref, out_hbm, out_ref, sems):
    totals = jnp.sum(jnp.sum(sums_ref[...], axis=0), axis=0, keepdims=True)
    lane = lax.broadcasted_iota(jnp.int32, totals.shape, 1)
    square = jnp.sum(jnp.where(lane == 0, totals, 0.0), axis=1, keepdims=True)
    curve = jnp.sum(jnp.where(lane == 1, totals, 0.0), axis=1, keepdims=True)
    step = square / (curve + epsilon)
    size = COMP * ROWS // BLOCKS
    stores = []
    for block in range(BLOCKS):
        rows = pl.ds(block * size, size)
        out_ref[rows, :] = jnp.maximum(stack_ref[rows, :] - step * grad_ref[rows, :], 0.0)
        stores.append(pltpu.make_async_copy(out_ref.at[rows], out_hbm.at[rows], sems.at[block]))
        stores[block].start()
    for store in stores:
        store.wait()


def exchange(values, axes, groups=None):
    return lax.all_to_all(
        values, axes, split_axis=0, concat_axis=0, axis_index_groups=groups, tiled=True
    )


def swap(values):
    return lax.ppermute(values, "frames", [(index, index ^ 1) for index in range(GROUP)])


def call(kernel, name, out_shape, in_specs, cost=None, vmem=24, **options):
    single = not isinstance(out_shape, tuple)
    options.setdefault("out_specs", VMEM if single else (VMEM,) * len(out_shape))
    return pl.pallas_call(
        kernel, out_shape=out_shape, in_specs=in_specs, name=name, cost_estimate=cost,
        compiler_params=pltpu.CompilerParams(vmem_limit_bytes=vmem * MIB), **options,
    )


def body(recording, template, shifts, support, temporal_init, spatial_init):
    movie = recording.reshape(LOCAL, HEIGHT, WIDTH)
    shift_table = shifts.transpose(1, 2, 0).reshape(2, LOCAL)
    index = lax.axis_index("frames")
    place = jnp.stack([index, lax.axis_index("planes"), index & 1]).astype(jnp.int32)
    payload = call(
        register_kernel, "register", f32(GROUP, LOCAL, ROWS, WIDTH), [HBM, HBM], vmem=60, out_specs=HBM,
        scratch_shapes=[
            pltpu.SMEM((2, LOCAL), jnp.int32),
            pltpu.VMEM((LOCAL, HEIGHT, WIDTH), jnp.float32),
            pltpu.VMEM((LOCAL, HEIGHT + 2 * MAXS, WIDTH), jnp.float32),
            pltpu.VMEM((LOCAL, GROUP, ROWS, WIDTH), jnp.float32),
            pltpu.SemaphoreType.DMA,
            pltpu.SemaphoreType.DMA((LOCAL,)),
            pltpu.SemaphoreType.DMA((LOCAL,)),
        ],
    )(shift_table, movie)
    series = exchange(payload, "frames").reshape(FRAMES * ROWS, WIDTH)
    spatial = spatial_init.reshape(COMP * ROWS, WIDTH)
    stack, spatial_high, spatial_low, mask, gram, picture, upper = call(
        spatial_kernel, "spatial",
        (f32(COMP * ROWS, WIDTH), b16(COMP, TILE), b16(COMP, TILE), f32(COMP, 128), f32(COMP, COMP),
         f32(ROWS, WIDTH), f32(8, 128)),
        [SMEM] + [VMEM] * 3,
        cost=pl.CostEstimate(flops=6 * COMP * COMP * TILE, bytes_accessed=4 << 20, transcendentals=0),
    )(place, spatial, support.T, template.reshape(HEIGHT, WIDTH))
    keep, give, high, low = call(
        cross_kernel, "cross",
        (f32(HALF, PACK), f32(HALF, PACK), b16(FRAMES, TILE), b16(FRAMES, TILE)),
        [VMEM] * 6,
    )(upper, series, picture, spatial_high, spatial_low, gram)

    def spread(kernel, name, values, copies):
        return call(kernel, name, f32(copies, *values.shape[1:]), [VMEM])(values)

    chips = [list(range(core, GROUP, 2)) for core in range(2)]
    part = call(add_kernel, "pair", f32(HALF, PACK), [VMEM] * 2)(keep, swap(give))
    part = exchange(part.reshape(GROUP // 2, LOCAL, PACK), "frames", chips)
    part = exchange(spread(spread_kernel, "spread", part, PLANES), "planes")
    mine = exchange(spread(weigh_kernel, "weigh", part, GROUP // 2), "frames", chips).reshape(HALF, PACK)
    temporal, grad, sums = call(
        step_kernel, "steps",
        (f32(FRAMES, COMP), f32(COMP * ROWS, WIDTH), f32(GROUP * PLANES, 1, 128)),
        [VMEM] * 10,
    )(upper, mine, swap(mine), temporal_init, jnp.asarray(trend_projector()), mask,
      spatial_high, spatial_low, high, low)
    sums = exchange(sums, ("frames", "planes")).reshape(GROUP, PLANES, 128)
    spatial = call(
        final_kernel, "update", f32(COMP * ROWS, WIDTH), [VMEM] * 3, out_specs=HBM,
        scratch_shapes=[
            pltpu.VMEM((COMP * ROWS, WIDTH), jnp.float32), pltpu.SemaphoreType.DMA((BLOCKS,)),
        ],
    )(sums, stack, grad)
    return (temporal, spatial.reshape(COMP, 1, TILE))


def solution(mesh):
    placed = (
        P("frames", "planes", None, None),
        P("planes", None, None),
        P("frames", "planes", None),
        P(),
        P(),
        P(None, "planes", "frames"),
    )
    return jax.shard_map(
        body,
        mesh=mesh,
        in_specs=placed,
        out_specs=(P(), P(None, "planes", "frames")),
        check_vma=False,
    )
```

```python
import numpy as np
import jax
import jax.numpy as jnp
from jax import lax
from jax.experimental import pallas as pl
from jax.experimental.pallas import tpu as pltpu
from jax.sharding import PartitionSpec as P

HEIGHT = 256
WIDTH = 128
COMP = 256
FRAMES = 256
PLANES = 8
TILE = 1024
NTREND = 16
GROUP = 32
LOCAL = 8
ROWS = TILE // WIDTH
PACK = 512
HALF = 128
MAXS = 16
BATCHES = ((0, 2), (2, 5), (5, 8))
BLOCKS = 8
epsilon = 1e-06

VMEM = pl.BlockSpec(memory_space=pltpu.VMEM)
SMEM = pl.BlockSpec(memory_space=pltpu.SMEM)
HBM = pl.BlockSpec(memory_space=pltpu.HBM)
MIB = 1024 * 1024
NN = ((1,), (0,))
NT = ((1,), (1,))


def f32(*shape):
    return jax.ShapeDtypeStruct(shape, jnp.float32)


def b16(*shape):
    return jax.ShapeDtypeStruct(shape, jnp.bfloat16)


def split(values):
    high = values.astype(jnp.bfloat16)
    return high, (values - high.astype(jnp.float32)).astype(jnp.bfloat16)


def product(left, right, dims):
    return lax.dot_general(left, right, (dims, ((), ())), preferred_element_type=jnp.float32)


def total(values):
    return jnp.sum(jnp.sum(values, axis=0, keepdims=True), axis=1, keepdims=True)


def dot(left, right, dims=NN):
    lefts = jnp.concatenate([left[0], left[0], left[1]], axis=1)
    rights = jnp.concatenate([right[0], right[1], right[0]], axis=dims[1][0])
    return product(lefts, rights, dims)


def trend_projector():
    times = np.arange(FRAMES)[:, None] + 0.5
    orders = np.arange(NTREND)[None, :]
    scales = np.where(orders == 0, np.sqrt(1.0 / FRAMES), np.sqrt(2.0 / FRAMES))
    basis = np.cos(np.pi * times * orders / FRAMES) * scales
    return (basis @ basis.T).astype(np.float32)


def register_kernel(shift_hbm, movie_hbm, out_hbm, shift_ref, movie_ref, wide_ref, moved_ref,
                    shift_sem, movie_sem, moved_sem):
    table = pltpu.make_async_copy(shift_hbm, shift_ref, shift_sem)
    table.start()
    copies = [
        pltpu.make_async_copy(movie_hbm.at[frame], movie_ref.at[frame], movie_sem.at[frame])
        for frame in range(LOCAL)
    ]
    for copy in copies:
        copy.start()
    table.wait()
    stores = []
    for start, stop in BATCHES:
        frames = range(start, stop)
        for frame in frames:
            copies[frame].wait()
        for frame in frames:
            picture = pltpu.roll(movie_ref[frame], jnp.mod(shift_ref[1, frame], WIDTH), 1)
            wide = wide_ref.at[frame]
            wide[pl.ds(0, MAXS), :] = picture[HEIGHT - MAXS:]
            wide[pl.ds(MAXS, HEIGHT), :] = picture
            wide[pl.ds(MAXS + HEIGHT, MAXS), :] = picture[:MAXS]
        for frame in frames:
            moved = wide_ref[frame, pl.ds(MAXS - shift_ref[0, frame], HEIGHT), :]
            moved_ref[frame] = moved.reshape(GROUP, ROWS, WIDTH)
        for frame in frames:
            store = pltpu.make_async_copy(moved_ref.at[frame], out_hbm.at[:, frame], moved_sem.at[frame])
            store.start()
            stores.append(store)
    for store in stores:
        store.wait()


def spatial_kernel(place_ref, spatial_ref, support_ref, template_ref,
                   stack_ref, high_ref, low_ref, mask_ref, pack_ref, picture_ref, upper_ref):
    upper_ref[...] = jnp.broadcast_to(jnp.where(place_ref[2] == 0, 1.0, 0.0), upper_ref.shape)
    start = pl.multiple_of(place_ref[0] * ROWS, ROWS)
    picture_ref[...] = template_ref[pl.ds(start, ROWS), :]
    tile = place_ref[1] * GROUP + place_ref[0]
    hits = jnp.where(support_ref[...] == tile, 1.0, 0.0)
    covered = jnp.max(hits, axis=0, keepdims=True)
    mask = jnp.transpose(jnp.broadcast_to(covered, (128, COMP)))
    mask_ref[...] = mask
    for row in range(ROWS):
        columns = slice(row * WIDTH, (row + 1) * WIDTH)
        spatial = spatial_ref[pl.ds(row, COMP, stride=ROWS), :] * mask
        stack_ref[pl.ds(row, COMP, stride=ROWS), :] = spatial
        high_ref[:, columns], low_ref[:, columns] = split(spatial)
    parts = (high_ref[...], low_ref[...])
    gram = dot(parts, parts, NT)
    pack_ref[:HALF, :] = gram[:HALF, :]
    pack_ref[HALF:, :HALF] = gram[HALF:, HALF:]
    pack_ref[HALF:, HALF:] = pltpu.roll(gram[:HALF, HALF:], HALF // 2, 1)


def cross_kernel(upper_ref, series_ref, picture_ref, spatial_high_ref, spatial_low_ref, gram_ref,
                 keep_ref, give_ref, high_ref, low_ref):
    picture = picture_ref[...]
    numerator = jnp.zeros((FRAMES, WIDTH), jnp.float32)
    energy = jnp.zeros((FRAMES, WIDTH), jnp.float32)
    for row in range(ROWS):
        columns = slice(row * WIDTH, (row + 1) * WIDTH)
        series = series_ref[pl.ds(row, FRAMES, stride=ROWS), :]
        high_ref[:, columns], low_ref[:, columns] = split(series)
        numerator += series * picture[row:row + 1]
        energy += series * series
    lane = lax.broadcasted_iota(jnp.int32, (FRAMES, 128), 1)
    extra = jnp.where(lane == HALF // 2, jnp.sum(numerator, axis=1, keepdims=True), jnp.sum(picture * picture))
    extra = jnp.where(lane == HALF // 2 + 1, jnp.sum(energy, axis=1, keepdims=True), extra)
    extra = jnp.where(lane < HALF // 2, gram_ref[:, HALF:], extra)
    cross = product(high_ref[...], spatial_high_ref[...], NT) + (
        product(high_ref[...], spatial_low_ref[...], NT) + product(low_ref[...], spatial_high_ref[...], NT)
    )
    upper = upper_ref[:1, :1] > 0.0
    for columns, values in (
        (slice(0, HALF), gram_ref[:, :HALF]), (slice(HALF, COMP), extra), (slice(COMP, PACK), cross)
    ):
        give_ref[:, columns] = jnp.where(upper, values[HALF:], values[:HALF])
        keep_ref[:, columns] = jnp.where(upper, values[:HALF], values[HALF:])


def add_kernel(left_ref, right_ref, out_ref):
    out_ref[...] = left_ref[...] + right_ref[...]


def spread_kernel(in_ref, out_ref):
    rows = jnp.sum(in_ref[...], axis=0)
    out_ref[...] = jnp.broadcast_to(rows[None], out_ref.shape)


def weigh_kernel(in_ref, out_ref):
    rows = jnp.sum(in_ref[...], axis=0)
    first = HALF + HALF // 2
    energy = rows[:, first + 1:first + 2] * rows[:, first + 2:first + 3]
    weight = rows[:, first:first + 1] / jnp.sqrt(energy + epsilon)
    column = lax.broadcasted_iota(jnp.int32, (LOCAL, PACK), 1)
    rows = jnp.where(column >= COMP, rows * weight, jnp.where(column == first, weight, rows))
    out_ref[...] = jnp.broadcast_to(rows[None], out_ref.shape)


def step_kernel(upper_ref, mine_ref, other_ref, temporal_ref, trend_ref, mask_ref,
                spatial_high_ref, spatial_low_ref, high_ref, low_ref,
                out_ref, grad_ref, sums_ref):
    first = upper_ref[:1, :1] > 0.0
    upper = jnp.where(first, mine_ref[...], other_ref[...])
    lower = jnp.where(first, other_ref[...], mine_ref[...])
    lane = lax.broadcasted_iota(jnp.int32, (HALF, HALF), 1)
    corner = jnp.where(
        lane < HALF // 2, upper[:, HALF:2 * HALF], pltpu.roll(lower[:, HALF:2 * HALF], HALF // 2, 1)
    )
    gram = split(jnp.concatenate([
        jnp.concatenate([upper[:, :HALF], corner], axis=1),
        jnp.concatenate([jnp.transpose(corner), lower[:, :HALF]], axis=1),
    ], axis=0))
    pack = jnp.concatenate([upper, lower], axis=0)
    weight = pack[:, HALF + HALF // 2:HALF + HALF // 2 + 1]
    cross = pack[:, COMP:]
    trend = split(trend_ref[...])
    temporal = temporal_ref[...]
    grad = dot(split(temporal), gram) + dot(trend, split(cross)) - cross
    step = total(grad * grad) / (total(grad * dot(split(grad), gram)) + epsilon)
    temporal = jnp.maximum(temporal - step * grad, 0.0)
    out_ref[...] = temporal
    flipped = jnp.transpose(temporal)
    parts = split(flipped)
    mixed = product(parts[0], parts[1], NT)
    temporal_gram = split(product(parts[0], parts[0], NT) + (mixed + jnp.transpose(mixed)))
    weight_row = jnp.transpose(jnp.broadcast_to(weight, (FRAMES, 128)))[:1]
    projector = split((flipped - dot(parts, trend)) * weight_row)
    spatial_grad = (
        dot(temporal_gram, (spatial_high_ref[...], spatial_low_ref[...]))
        - dot(projector, (high_ref[...], low_ref[...]))
    )
    mask = mask_ref[...]
    spatial_grad = jnp.concatenate(
        [spatial_grad[:, row * WIDTH:(row + 1) * WIDTH] * mask for row in range(ROWS)], axis=1
    )
    for row in range(ROWS):
        grad_ref[pl.ds(row, COMP, stride=ROWS), :] = spatial_grad[:, row * WIDTH:(row + 1) * WIDTH]
    square = total(spatial_grad * spatial_grad)
    curve = total(spatial_grad * dot(temporal_gram, split(spatial_grad)))
    lane = lax.broadcasted_iota(jnp.int32, sums_ref.shape, 2)
    sums_ref[...] = jnp.where(lane == 0, square, jnp.where(lane == 1, curve, 0.0))


def final_kernel(sums_ref, stack_ref, grad_ref, out_hbm, out_ref, sems):
    sums = jnp.sum(sums_ref[...], axis=0)
    lane = lax.broadcasted_iota(jnp.int32, sums.shape, 1)
    square = total(jnp.where(lane == 0, sums, 0.0))
    curve = total(jnp.where(lane == 1, sums, 0.0))
    step = square / (curve + epsilon)
    size = COMP * ROWS // BLOCKS
    stores = []
    for block in range(BLOCKS):
        rows = pl.ds(block * size, size)
        out_ref[rows, :] = jnp.maximum(stack_ref[rows, :] - step * grad_ref[rows, :], 0.0)
        stores.append(pltpu.make_async_copy(out_ref.at[rows], out_hbm.at[rows], sems.at[block]))
        stores[block].start()
    for store in stores:
        store.wait()


def exchange(values, axes, groups=None):
    return lax.all_to_all(
        values, axes, split_axis=0, concat_axis=0, axis_index_groups=groups, tiled=True
    )


def swap(values):
    return lax.ppermute(values, "frames", [(index, index ^ 1) for index in range(GROUP)])


def call(kernel, name, out_shape, in_specs, cost=None, vmem=24, **options):
    single = not isinstance(out_shape, tuple)
    options.setdefault("out_specs", VMEM if single else (VMEM,) * len(out_shape))
    return pl.pallas_call(
        kernel, out_shape=out_shape, in_specs=in_specs, name=name, cost_estimate=cost,
        compiler_params=pltpu.CompilerParams(vmem_limit_bytes=vmem * MIB), **options,
    )


def body(recording, template, shifts, support, temporal_init, spatial_init):
    movie = recording.reshape(LOCAL, HEIGHT, WIDTH)
    shift_table = shifts.transpose(1, 2, 0).reshape(2, LOCAL)
    index = lax.axis_index("frames")
    place = jnp.stack([index, lax.axis_index("planes"), index & 1]).astype(jnp.int32)
    payload = call(
        register_kernel, "register", f32(GROUP, LOCAL, ROWS, WIDTH), [HBM, HBM], vmem=60, out_specs=HBM,
        scratch_shapes=[
            pltpu.SMEM((2, LOCAL), jnp.int32),
            pltpu.VMEM((LOCAL, HEIGHT, WIDTH), jnp.float32),
            pltpu.VMEM((LOCAL, HEIGHT + 2 * MAXS, WIDTH), jnp.float32),
            pltpu.VMEM((LOCAL, GROUP, ROWS, WIDTH), jnp.float32),
            pltpu.SemaphoreType.DMA,
            pltpu.SemaphoreType.DMA((LOCAL,)),
            pltpu.SemaphoreType.DMA((LOCAL,)),
        ],
    )(shift_table, movie)
    series = exchange(payload, "frames").reshape(FRAMES * ROWS, WIDTH)
    spatial = spatial_init.reshape(COMP * ROWS, WIDTH)
    stack, spatial_high, spatial_low, mask, gram, picture, upper = call(
        spatial_kernel, "spatial",
        (f32(COMP * ROWS, WIDTH), b16(COMP, TILE), b16(COMP, TILE), f32(COMP, 128), f32(COMP, COMP),
         f32(ROWS, WIDTH), f32(8, 128)),
        [SMEM] + [VMEM] * 3,
        cost=pl.CostEstimate(flops=6 * COMP * COMP * TILE, bytes_accessed=4 << 20, transcendentals=0),
    )(place, spatial, support.T, template.reshape(HEIGHT, WIDTH))
    keep, give, high, low = call(
        cross_kernel, "cross",
        (f32(HALF, PACK), f32(HALF, PACK), b16(FRAMES, TILE), b16(FRAMES, TILE)),
        [VMEM] * 6,
    )(upper, series, picture, spatial_high, spatial_low, gram)

    def spread(kernel, name, values, copies):
        return call(kernel, name, f32(copies, *values.shape[1:]), [VMEM])(values)

    chips = [list(range(core, GROUP, 2)) for core in range(2)]
    part = call(add_kernel, "pair", f32(HALF, PACK), [VMEM] * 2)(keep, swap(give))
    part = exchange(part.reshape(GROUP // 2, LOCAL, PACK), "frames", chips)
    part = exchange(spread(spread_kernel, "spread", part, PLANES), "planes")
    mine = exchange(spread(weigh_kernel, "weigh", part, GROUP // 2), "frames", chips).reshape(HALF, PACK)
    temporal, grad, sums = call(
        step_kernel, "steps",
        (f32(FRAMES, COMP), f32(COMP * ROWS, WIDTH), f32(GROUP, PLANES, 128)),
        [VMEM] * 10,
    )(upper, mine, swap(mine), temporal_init, jnp.asarray(trend_projector()), mask,
      spatial_high, spatial_low, high, low)
    sums = exchange(sums.reshape(GROUP * PLANES, 1, 128), ("frames", "planes"))
    spatial = call(
        final_kernel, "update", f32(COMP * ROWS, WIDTH), [VMEM] * 3, out_specs=HBM,
        scratch_shapes=[
            pltpu.VMEM((COMP * ROWS, WIDTH), jnp.float32), pltpu.SemaphoreType.DMA((BLOCKS,)),
        ],
    )(sums.reshape(GROUP, PLANES, 128), stack, grad)
    return (temporal, spatial.reshape(COMP, 1, TILE))


def solution(mesh):
    placed = (
        P("frames", "planes", None, None),
        P("planes", None, None),
        P("frames", "planes", None),
        P(),
        P(),
        P(None, "planes", "frames"),
    )
    return jax.shard_map(
        body,
        mesh=mesh,
        in_specs=placed,
        out_specs=(P(), P(None, "planes", "frames")),
        check_vma=False,
    )
```

```python
import numpy as np
import jax
import jax.numpy as jnp
from jax import lax
from jax.experimental import pallas as pl
from jax.experimental.pallas import tpu as pltpu
from jax.sharding import PartitionSpec as P

HEIGHT = 256
WIDTH = 128
COMP = 256
FRAMES = 256
PLANES = 8
TILE = 1024
NTREND = 16
GROUP = 32
LOCAL = 8
ROWS = TILE // WIDTH
PACK = 512
HALF = 128
MAXS = 16
BATCHES = ((0, 2), (2, 5), (5, 8))
BLOCKS = 8
epsilon = 1e-06

GRID = np.arange(GROUP * PLANES).reshape(4, 4, 2, PLANES)
PLANE = (GRID[..., 0] // PLANES).transpose(1, 0, 2).flatten().tolist()
CHIPS = (GRID[..., 0] // PLANES).transpose(2, 1, 0).reshape(2, 16).tolist()
ALL = GRID.transpose(3, 2, 0, 1).flatten().tolist()

VMEM = pl.BlockSpec(memory_space=pltpu.VMEM)
SMEM = pl.BlockSpec(memory_space=pltpu.SMEM)
HBM = pl.BlockSpec(memory_space=pltpu.HBM)
MIB = 1024 * 1024
NN = ((1,), (0,))
NT = ((1,), (1,))


def f32(*shape):
    return jax.ShapeDtypeStruct(shape, jnp.float32)


def b16(*shape):
    return jax.ShapeDtypeStruct(shape, jnp.bfloat16)


def split(values):
    high = values.astype(jnp.bfloat16)
    return high, (values - high.astype(jnp.float32)).astype(jnp.bfloat16)


def product(left, right, dims):
    return lax.dot_general(left, right, (dims, ((), ())), preferred_element_type=jnp.float32)


def total(values):
    return jnp.sum(jnp.sum(values, axis=0, keepdims=True), axis=1, keepdims=True)


def dot(left, right, dims=NN):
    lefts = jnp.concatenate([left[0], left[0], left[1]], axis=1)
    rights = jnp.concatenate([right[0], right[1], right[0]], axis=dims[1][0])
    return product(lefts, rights, dims)


def trend_projector():
    times = np.arange(FRAMES)[:, None] + 0.5
    orders = np.arange(NTREND)[None, :]
    scales = np.where(orders == 0, np.sqrt(1.0 / FRAMES), np.sqrt(2.0 / FRAMES))
    basis = np.cos(np.pi * times * orders / FRAMES) * scales
    return (basis @ basis.T).astype(np.float32)


def register_kernel(shift_hbm, movie_hbm, out_hbm, shift_ref, movie_ref, wide_ref, moved_ref,
                    shift_sem, movie_sem, moved_sem):
    table = pltpu.make_async_copy(shift_hbm, shift_ref, shift_sem)
    table.start()
    copies = [
        pltpu.make_async_copy(movie_hbm.at[frame], movie_ref.at[frame], movie_sem.at[frame])
        for frame in range(LOCAL)
    ]
    for copy in copies:
        copy.start()
    table.wait()
    stores = []
    for start, stop in BATCHES:
        frames = range(start, stop)
        for frame in frames:
            copies[frame].wait()
        for frame in frames:
            picture = pltpu.roll(movie_ref[frame], jnp.mod(shift_ref[1, frame], WIDTH), 1)
            wide = wide_ref.at[frame]
            wide[pl.ds(0, MAXS), :] = picture[HEIGHT - MAXS:]
            wide[pl.ds(MAXS, HEIGHT), :] = picture
            wide[pl.ds(MAXS + HEIGHT, MAXS), :] = picture[:MAXS]
        for frame in frames:
            moved = wide_ref[frame, pl.ds(MAXS - shift_ref[0, frame], HEIGHT), :]
            for slot, block in enumerate(PLANE):
                moved_ref[frame, slot] = moved[block * ROWS:(block + 1) * ROWS]
        for frame in frames:
            store = pltpu.make_async_copy(moved_ref.at[frame], out_hbm.at[:, frame], moved_sem.at[frame])
            store.start()
            stores.append(store)
    for store in stores:
        store.wait()


def spatial_kernel(place_ref, spatial_ref, support_ref, template_ref,
                   stack_ref, high_ref, low_ref, mask_ref, pack_ref, picture_ref, upper_ref):
    upper_ref[...] = jnp.broadcast_to(jnp.where(place_ref[2] == 0, 1.0, 0.0), upper_ref.shape)
    start = pl.multiple_of(place_ref[0] * ROWS, ROWS)
    picture_ref[...] = template_ref[pl.ds(start, ROWS), :]
    tile = place_ref[1] * GROUP + place_ref[0]
    hits = jnp.where(support_ref[...] == tile, 1.0, 0.0)
    covered = jnp.max(hits, axis=0, keepdims=True)
    mask = jnp.transpose(jnp.broadcast_to(covered, (128, COMP)))
    mask_ref[...] = mask
    for row in range(ROWS):
        columns = slice(row * WIDTH, (row + 1) * WIDTH)
        spatial = spatial_ref[pl.ds(row, COMP, stride=ROWS), :] * mask
        stack_ref[pl.ds(row, COMP, stride=ROWS), :] = spatial
        high_ref[:, columns], low_ref[:, columns] = split(spatial)
    parts = (high_ref[...], low_ref[...])
    gram = dot(parts, parts, NT)
    pack_ref[:HALF, :] = gram[:HALF, :]
    pack_ref[HALF:, :HALF] = gram[HALF:, HALF:]
    pack_ref[HALF:, HALF:] = pltpu.roll(gram[:HALF, HALF:], HALF // 2, 1)


def cross_kernel(upper_ref, series_ref, picture_ref, spatial_high_ref, spatial_low_ref, gram_ref,
                 keep_ref, give_ref, high_ref, low_ref):
    picture = picture_ref[...]
    numerator = jnp.zeros((FRAMES, WIDTH), jnp.float32)
    energy = jnp.zeros((FRAMES, WIDTH), jnp.float32)
    for row in range(ROWS):
        columns = slice(row * WIDTH, (row + 1) * WIDTH)
        series = jnp.concatenate([
            series_ref[pl.ds(PLANE.index(block) * LOCAL * ROWS + row, LOCAL, stride=ROWS), :]
            for block in range(GROUP)
        ], axis=0)
        high_ref[:, columns], low_ref[:, columns] = split(series)
        numerator += series * picture[row:row + 1]
        energy += series * series
    lane = lax.broadcasted_iota(jnp.int32, (FRAMES, 128), 1)
    extra = jnp.where(lane == HALF // 2, jnp.sum(numerator, axis=1, keepdims=True), jnp.sum(picture * picture))
    extra = jnp.where(lane == HALF // 2 + 1, jnp.sum(energy, axis=1, keepdims=True), extra)
    extra = jnp.where(lane < HALF // 2, gram_ref[:, HALF:], extra)
    cross = product(high_ref[...], spatial_high_ref[...], NT) + (
        product(high_ref[...], spatial_low_ref[...], NT) + product(low_ref[...], spatial_high_ref[...], NT)
    )
    upper = upper_ref[:1, :1] > 0.0
    for columns, values in (
        (slice(0, HALF), gram_ref[:, :HALF]), (slice(HALF, COMP), extra), (slice(COMP, PACK), cross)
    ):
        give_ref[:, columns] = jnp.where(upper, values[HALF:], values[:HALF])
        keep_ref[:, columns] = jnp.where(upper, values[:HALF], values[HALF:])


def add_kernel(left_ref, right_ref, out_ref):
    out_ref[...] = left_ref[...] + right_ref[...]


def spread_kernel(in_ref, out_ref):
    rows = jnp.sum(in_ref[...], axis=0)
    out_ref[...] = jnp.broadcast_to(rows[None], out_ref.shape)


def weigh_kernel(in_ref, out_ref):
    rows = jnp.sum(in_ref[...], axis=0)
    first = HALF + HALF // 2
    energy = rows[:, first + 1:first + 2] * rows[:, first + 2:first + 3]
    weight = rows[:, first:first + 1] / jnp.sqrt(energy + epsilon)
    column = lax.broadcasted_iota(jnp.int32, (LOCAL, PACK), 1)
    rows = jnp.where(column >= COMP, rows * weight, jnp.where(column == first, weight, rows))
    out_ref[...] = jnp.broadcast_to(rows[None], out_ref.shape)


def step_kernel(upper_ref, mine_ref, other_ref, temporal_ref, trend_ref, mask_ref,
                spatial_high_ref, spatial_low_ref, high_ref, low_ref,
                out_ref, grad_ref, sums_ref):
    first = upper_ref[:1, :1] > 0.0
    upper = jnp.where(first, mine_ref[...], other_ref[...])
    lower = jnp.where(first, other_ref[...], mine_ref[...])
    lane = lax.broadcasted_iota(jnp.int32, (HALF, HALF), 1)
    corner = jnp.where(
        lane < HALF // 2, upper[:, HALF:2 * HALF], pltpu.roll(lower[:, HALF:2 * HALF], HALF // 2, 1)
    )
    gram = split(jnp.concatenate([
        jnp.concatenate([upper[:, :HALF], corner], axis=1),
        jnp.concatenate([jnp.transpose(corner), lower[:, :HALF]], axis=1),
    ], axis=0))
    pack = jnp.concatenate([upper, lower], axis=0)
    weight = pack[:, HALF + HALF // 2:HALF + HALF // 2 + 1]
    cross = pack[:, COMP:]
    trend = split(trend_ref[...])
    temporal = temporal_ref[...]
    grad = dot(split(temporal), gram) + dot(trend, split(cross)) - cross
    step = total(grad * grad) / (total(grad * dot(split(grad), gram)) + epsilon)
    temporal = jnp.maximum(temporal - step * grad, 0.0)
    out_ref[...] = temporal
    flipped = jnp.transpose(temporal)
    parts = split(flipped)
    mixed = product(parts[0], parts[1], NT)
    temporal_gram = split(product(parts[0], parts[0], NT) + (mixed + jnp.transpose(mixed)))
    weight_row = jnp.transpose(jnp.broadcast_to(weight, (FRAMES, 128)))[:1]
    projector = split((flipped - dot(parts, trend)) * weight_row)
    spatial_grad = (
        dot(temporal_gram, (spatial_high_ref[...], spatial_low_ref[...]))
        - dot(projector, (high_ref[...], low_ref[...]))
    )
    mask = mask_ref[...]
    spatial_grad = jnp.concatenate(
        [spatial_grad[:, row * WIDTH:(row + 1) * WIDTH] * mask for row in range(ROWS)], axis=1
    )
    for row in range(ROWS):
        grad_ref[pl.ds(row, COMP, stride=ROWS), :] = spatial_grad[:, row * WIDTH:(row + 1) * WIDTH]
    square = total(spatial_grad * spatial_grad)
    curve = total(spatial_grad * dot(temporal_gram, split(spatial_grad)))
    lane = lax.broadcasted_iota(jnp.int32, sums_ref.shape, 2)
    sums_ref[...] = jnp.where(lane == 0, square, jnp.where(lane == 1, curve, 0.0))


def final_kernel(sums_ref, stack_ref, grad_ref, out_hbm, out_ref, sems):
    sums = jnp.sum(sums_ref[...], axis=0)
    lane = lax.broadcasted_iota(jnp.int32, sums.shape, 1)
    square = total(jnp.where(lane == 0, sums, 0.0))
    curve = total(jnp.where(lane == 1, sums, 0.0))
    step = square / (curve + epsilon)
    size = COMP * ROWS // BLOCKS
    stores = []
    for block in range(BLOCKS):
        rows = pl.ds(block * size, size)
        out_ref[rows, :] = jnp.maximum(stack_ref[rows, :] - step * grad_ref[rows, :], 0.0)
        stores.append(pltpu.make_async_copy(out_ref.at[rows], out_hbm.at[rows], sems.at[block]))
        stores[block].start()
    for store in stores:
        store.wait()


def exchange(values, axes, groups=None):
    return lax.all_to_all(
        values, axes, split_axis=0, concat_axis=0, axis_index_groups=groups, tiled=True
    )


def swap(values):
    return lax.ppermute(values, "frames", [(index, index ^ 1) for index in range(GROUP)])


def call(kernel, name, out_shape, in_specs, cost=None, vmem=24, **options):
    single = not isinstance(out_shape, tuple)
    options.setdefault("out_specs", VMEM if single else (VMEM,) * len(out_shape))
    return pl.pallas_call(
        kernel, out_shape=out_shape, in_specs=in_specs, name=name, cost_estimate=cost,
        compiler_params=pltpu.CompilerParams(vmem_limit_bytes=vmem * MIB), **options,
    )


def body(recording, template, shifts, support, temporal_init, spatial_init):
    movie = recording.reshape(LOCAL, HEIGHT, WIDTH)
    shift_table = shifts.transpose(1, 2, 0).reshape(2, LOCAL)
    index = lax.axis_index("frames")
    place = jnp.stack([index, lax.axis_index("planes"), index & 1]).astype(jnp.int32)
    payload = call(
        register_kernel, "register", f32(GROUP, LOCAL, ROWS, WIDTH), [HBM, HBM], vmem=60, out_specs=HBM,
        scratch_shapes=[
            pltpu.SMEM((2, LOCAL), jnp.int32),
            pltpu.VMEM((LOCAL, HEIGHT, WIDTH), jnp.float32),
            pltpu.VMEM((LOCAL, HEIGHT + 2 * MAXS, WIDTH), jnp.float32),
            pltpu.VMEM((LOCAL, GROUP, ROWS, WIDTH), jnp.float32),
            pltpu.SemaphoreType.DMA,
            pltpu.SemaphoreType.DMA((LOCAL,)),
            pltpu.SemaphoreType.DMA((LOCAL,)),
        ],
    )(shift_table, movie)
    series = exchange(payload, "frames", [PLANE]).reshape(FRAMES * ROWS, WIDTH)
    spatial = spatial_init.reshape(COMP * ROWS, WIDTH)
    stack, spatial_high, spatial_low, mask, gram, picture, upper = call(
        spatial_kernel, "spatial",
        (f32(COMP * ROWS, WIDTH), b16(COMP, TILE), b16(COMP, TILE), f32(COMP, 128), f32(COMP, COMP),
         f32(ROWS, WIDTH), f32(8, 128)),
        [SMEM] + [VMEM] * 3,
        cost=pl.CostEstimate(flops=6 * COMP * COMP * TILE, bytes_accessed=4 << 20, transcendentals=0),
    )(place, spatial, support.T, template.reshape(HEIGHT, WIDTH))
    keep, give, high, low = call(
        cross_kernel, "cross",
        (f32(HALF, PACK), f32(HALF, PACK), b16(FRAMES, TILE), b16(FRAMES, TILE)),
        [VMEM] * 6,
    )(upper, series, picture, spatial_high, spatial_low, gram)

    def spread(kernel, name, values, copies):
        return call(kernel, name, f32(copies, *values.shape[1:]), [VMEM])(values)

    part = call(add_kernel, "pair", f32(HALF, PACK), [VMEM] * 2)(keep, swap(give))
    part = exchange(part.reshape(GROUP // 2, LOCAL, PACK), "frames", CHIPS)
    part = exchange(spread(spread_kernel, "spread", part, PLANES), "planes")
    mine = exchange(spread(weigh_kernel, "weigh", part, GROUP // 2), "frames", CHIPS).reshape(HALF, PACK)
    temporal, grad, sums = call(
        step_kernel, "steps",
        (f32(FRAMES, COMP), f32(COMP * ROWS, WIDTH), f32(GROUP, PLANES, 128)),
        [VMEM] * 10,
    )(upper, mine, swap(mine), temporal_init, jnp.asarray(trend_projector()), mask,
      spatial_high, spatial_low, high, low)
    sums = exchange(sums.reshape(GROUP * PLANES, 1, 128), ("frames", "planes"), [ALL])
    spatial = call(
        final_kernel, "update", f32(COMP * ROWS, WIDTH), [VMEM] * 3, out_specs=HBM,
        scratch_shapes=[
            pltpu.VMEM((COMP * ROWS, WIDTH), jnp.float32), pltpu.SemaphoreType.DMA((BLOCKS,)),
        ],
    )(sums.reshape(GROUP, PLANES, 128), stack, grad)
    return (temporal, spatial.reshape(COMP, 1, TILE))


def solution(mesh):
    placed = (
        P("frames", "planes", None, None),
        P("planes", None, None),
        P("frames", "planes", None),
        P(),
        P(),
        P(None, "planes", "frames"),
    )
    return jax.shard_map(
        body,
        mesh=mesh,
        in_specs=placed,
        out_specs=(P(), P(None, "planes", "frames")),
        check_vma=False,
    )
```

```python
import numpy as np
import jax
import jax.numpy as jnp
from jax import lax
from jax.experimental import pallas as pl
from jax.experimental.pallas import tpu as pltpu
from jax.sharding import PartitionSpec as P

HEIGHT = 256
WIDTH = 128
COMP = 256
FRAMES = 256
PLANES = 8
TILE = 1024
NTREND = 16
GROUP = 32
LOCAL = 8
ROWS = TILE // WIDTH
PACK = 512
HALF = 128
MAXS = 16
BATCHES = ((0, 2), (2, 5), (5, 8))
BLOCKS = 8
epsilon = 1e-06

VMEM = pl.BlockSpec(memory_space=pltpu.VMEM)
SMEM = pl.BlockSpec(memory_space=pltpu.SMEM)
HBM = pl.BlockSpec(memory_space=pltpu.HBM)
MIB = 1024 * 1024
NN = ((1,), (0,))
NT = ((1,), (1,))


def f32(*shape):
    return jax.ShapeDtypeStruct(shape, jnp.float32)


def b16(*shape):
    return jax.ShapeDtypeStruct(shape, jnp.bfloat16)


def split(values):
    high = values.astype(jnp.bfloat16)
    return high, (values - high.astype(jnp.float32)).astype(jnp.bfloat16)


def product(left, right, dims):
    return lax.dot_general(left, right, (dims, ((), ())), preferred_element_type=jnp.float32)


def total(values):
    return jnp.sum(jnp.sum(values, axis=0, keepdims=True), axis=1, keepdims=True)


def dot(left, right, dims=NN):
    lefts = jnp.concatenate([left[0], left[0], left[1]], axis=1)
    rights = jnp.concatenate([right[0], right[1], right[0]], axis=dims[1][0])
    return product(lefts, rights, dims)


def trend_projector():
    times = np.arange(FRAMES)[:, None] + 0.5
    orders = np.arange(NTREND)[None, :]
    scales = np.where(orders == 0, np.sqrt(1.0 / FRAMES), np.sqrt(2.0 / FRAMES))
    basis = np.cos(np.pi * times * orders / FRAMES) * scales
    return (basis @ basis.T).astype(np.float32)


def register_kernel(shift_hbm, movie_hbm, out_hbm, shift_ref, movie_ref, wide_ref, moved_ref,
                    shift_sem, movie_sem, moved_sem):
    table = pltpu.make_async_copy(shift_hbm, shift_ref, shift_sem)
    table.start()
    copies = [
        pltpu.make_async_copy(movie_hbm.at[frame], movie_ref.at[frame], movie_sem.at[frame])
        for frame in range(LOCAL)
    ]
    for copy in copies:
        copy.start()
    table.wait()
    stores = []
    for start, stop in BATCHES:
        frames = range(start, stop)
        for frame in frames:
            copies[frame].wait()
        for frame in frames:
            picture = pltpu.roll(movie_ref[frame], jnp.mod(shift_ref[1, frame], WIDTH), 1)
            wide = wide_ref.at[frame]
            wide[pl.ds(0, MAXS), :] = picture[HEIGHT - MAXS:]
            wide[pl.ds(MAXS, HEIGHT), :] = picture
            wide[pl.ds(MAXS + HEIGHT, MAXS), :] = picture[:MAXS]
        for frame in frames:
            moved = wide_ref[frame, pl.ds(MAXS - shift_ref[0, frame], HEIGHT), :]
            moved_ref[frame] = moved.reshape(GROUP, ROWS, WIDTH)
        for frame in frames:
            store = pltpu.make_async_copy(moved_ref.at[frame], out_hbm.at[:, frame], moved_sem.at[frame])
            store.start()
            stores.append(store)
    for store in stores:
        store.wait()


def spatial_kernel(place_ref, spatial_ref, support_ref, template_ref,
                   stack_ref, high_ref, low_ref, mask_ref, pack_ref, picture_ref, upper_ref):
    upper_ref[...] = jnp.broadcast_to(jnp.where(place_ref[2] == 0, 1.0, 0.0), upper_ref.shape)
    start = pl.multiple_of(place_ref[0] * ROWS, ROWS)
    picture_ref[...] = template_ref[pl.ds(start, ROWS), :]
    tile = place_ref[1] * GROUP + place_ref[0]
    hits = jnp.where(support_ref[...] == tile, 1.0, 0.0)
    covered = jnp.max(hits, axis=0, keepdims=True)
    mask = jnp.transpose(jnp.broadcast_to(covered, (128, COMP)))
    mask_ref[...] = mask
    for row in range(ROWS):
        columns = slice(row * WIDTH, (row + 1) * WIDTH)
        spatial = spatial_ref[pl.ds(row, COMP, stride=ROWS), :] * mask
        stack_ref[pl.ds(row, COMP, stride=ROWS), :] = spatial
        high_ref[:, columns], low_ref[:, columns] = split(spatial)
    parts = (high_ref[...], low_ref[...])
    gram = dot(parts, parts, NT)
    pack_ref[:HALF, :] = gram[:HALF, :]
    pack_ref[HALF:, :HALF] = gram[HALF:, HALF:]
    pack_ref[HALF:, HALF:] = pltpu.roll(gram[:HALF, HALF:], HALF // 2, 1)


def cross_kernel(upper_ref, series_ref, picture_ref, spatial_high_ref, spatial_low_ref, gram_ref,
                 keep_ref, give_ref, high_ref, low_ref):
    picture = picture_ref[...]
    numerator = jnp.zeros((FRAMES, WIDTH), jnp.float32)
    energy = jnp.zeros((FRAMES, WIDTH), jnp.float32)
    for row in range(ROWS):
        columns = slice(row * WIDTH, (row + 1) * WIDTH)
        series = series_ref[pl.ds(row, FRAMES, stride=ROWS), :]
        high_ref[:, columns], low_ref[:, columns] = split(series)
        numerator += series * picture[row:row + 1]
        energy += series * series
    lane = lax.broadcasted_iota(jnp.int32, (FRAMES, 128), 1)
    extra = jnp.where(lane == HALF // 2, jnp.sum(numerator, axis=1, keepdims=True), jnp.sum(picture * picture))
    extra = jnp.where(lane == HALF // 2 + 1, jnp.sum(energy, axis=1, keepdims=True), extra)
    extra = jnp.where(lane < HALF // 2, gram_ref[:, HALF:], extra)
    cross = product(high_ref[...], spatial_high_ref[...], NT) + (
        product(high_ref[...], spatial_low_ref[...], NT) + product(low_ref[...], spatial_high_ref[...], NT)
    )
    upper = upper_ref[:1, :1] > 0.0
    for columns, values in (
        (slice(0, HALF), gram_ref[:, :HALF]), (slice(HALF, COMP), extra), (slice(COMP, PACK), cross)
    ):
        give_ref[:, columns] = jnp.where(upper, values[HALF:], values[:HALF])
        keep_ref[:, columns] = jnp.where(upper, values[:HALF], values[HALF:])


def add_kernel(left_ref, right_ref, out_ref):
    out_ref[...] = left_ref[...] + right_ref[...]


def spread_kernel(in_ref, out_ref):
    rows = jnp.sum(in_ref[...], axis=0)
    out_ref[...] = jnp.broadcast_to(rows[None], out_ref.shape)


def weigh_kernel(in_ref, out_ref):
    rows = jnp.sum(in_ref[...], axis=0)
    first = HALF + HALF // 2
    energy = rows[:, first + 1:first + 2] * rows[:, first + 2:first + 3]
    weight = rows[:, first:first + 1] / jnp.sqrt(energy + epsilon)
    column = lax.broadcasted_iota(jnp.int32, (LOCAL, PACK), 1)
    rows = jnp.where(column >= COMP, rows * weight, jnp.where(column == first, weight, rows))
    out_ref[...] = jnp.broadcast_to(rows[None], out_ref.shape)


def step_kernel(upper_ref, mine_ref, other_ref, temporal_ref, trend_ref, mask_ref,
                spatial_high_ref, spatial_low_ref, high_ref, low_ref,
                out_ref, grad_ref, sums_ref):
    first = upper_ref[:1, :1] > 0.0
    upper = jnp.where(first, mine_ref[...], other_ref[...])
    lower = jnp.where(first, other_ref[...], mine_ref[...])
    lane = lax.broadcasted_iota(jnp.int32, (HALF, HALF), 1)
    corner = jnp.where(
        lane < HALF // 2, upper[:, HALF:2 * HALF], pltpu.roll(lower[:, HALF:2 * HALF], HALF // 2, 1)
    )
    gram = split(jnp.concatenate([
        jnp.concatenate([upper[:, :HALF], corner], axis=1),
        jnp.concatenate([jnp.transpose(corner), lower[:, :HALF]], axis=1),
    ], axis=0))
    pack = jnp.concatenate([upper, lower], axis=0)
    weight = pack[:, HALF + HALF // 2:HALF + HALF // 2 + 1]
    cross = pack[:, COMP:]
    trend = split(trend_ref[...])
    temporal = temporal_ref[...]
    grad = dot(split(temporal), gram) + dot(trend, split(cross)) - cross
    step = total(grad * grad) / (total(grad * dot(split(grad), gram)) + epsilon)
    temporal = jnp.maximum(temporal - step * grad, 0.0)
    out_ref[...] = temporal
    flipped = jnp.transpose(temporal)
    parts = split(flipped)
    mixed = product(parts[0], parts[1], NT)
    temporal_gram_whole = product(parts[0], parts[0], NT) + (mixed + jnp.transpose(mixed))
    temporal_gram = split(temporal_gram_whole)
    weight_row = jnp.transpose(jnp.broadcast_to(weight, (FRAMES, 128)))[:1]
    projector = split((flipped - dot(parts, trend)) * weight_row)
    spatial_grad = (
        dot(temporal_gram, (spatial_high_ref[...], spatial_low_ref[...]))
        - dot(projector, (high_ref[...], low_ref[...]))
    )
    mask = mask_ref[...]
    spatial_grad = jnp.concatenate(
        [spatial_grad[:, row * WIDTH:(row + 1) * WIDTH] * mask for row in range(ROWS)], axis=1
    )
    for row in range(ROWS):
        grad_ref[pl.ds(row, COMP, stride=ROWS), :] = spatial_grad[:, row * WIDTH:(row + 1) * WIDTH]
    square = total(spatial_grad * spatial_grad)
    high, low = split(spatial_grad)
    curve = total(temporal_gram_whole * (product(high, high, NT) + 2.0 * product(high, low, NT)))
    lane = lax.broadcasted_iota(jnp.int32, sums_ref.shape, 2)
    sums_ref[...] = jnp.where(lane == 0, square, jnp.where(lane == 1, curve, 0.0))


def final_kernel(sums_ref, stack_ref, grad_ref, out_hbm, out_ref, sems):
    sums = jnp.sum(sums_ref[...], axis=0)
    lane = lax.broadcasted_iota(jnp.int32, sums.shape, 1)
    square = total(jnp.where(lane == 0, sums, 0.0))
    curve = total(jnp.where(lane == 1, sums, 0.0))
    step = square / (curve + epsilon)
    size = COMP * ROWS // BLOCKS
    stores = []
    for block in range(BLOCKS):
        rows = pl.ds(block * size, size)
        out_ref[rows, :] = jnp.maximum(stack_ref[rows, :] - step * grad_ref[rows, :], 0.0)
        stores.append(pltpu.make_async_copy(out_ref.at[rows], out_hbm.at[rows], sems.at[block]))
        stores[block].start()
    for store in stores:
        store.wait()


def exchange(values, axes, groups=None):
    return lax.all_to_all(
        values, axes, split_axis=0, concat_axis=0, axis_index_groups=groups, tiled=True
    )


def swap(values):
    return lax.ppermute(values, "frames", [(index, index ^ 1) for index in range(GROUP)])


def call(kernel, name, out_shape, in_specs, cost=None, vmem=24, **options):
    single = not isinstance(out_shape, tuple)
    options.setdefault("out_specs", VMEM if single else (VMEM,) * len(out_shape))
    return pl.pallas_call(
        kernel, out_shape=out_shape, in_specs=in_specs, name=name, cost_estimate=cost,
        compiler_params=pltpu.CompilerParams(vmem_limit_bytes=vmem * MIB), **options,
    )


def body(recording, template, shifts, support, temporal_init, spatial_init):
    movie = recording.reshape(LOCAL, HEIGHT, WIDTH)
    shift_table = shifts.transpose(1, 2, 0).reshape(2, LOCAL)
    index = lax.axis_index("frames")
    place = jnp.stack([index, lax.axis_index("planes"), index & 1]).astype(jnp.int32)
    payload = call(
        register_kernel, "register", f32(GROUP, LOCAL, ROWS, WIDTH), [HBM, HBM], vmem=60, out_specs=HBM,
        scratch_shapes=[
            pltpu.SMEM((2, LOCAL), jnp.int32),
            pltpu.VMEM((LOCAL, HEIGHT, WIDTH), jnp.float32),
            pltpu.VMEM((LOCAL, HEIGHT + 2 * MAXS, WIDTH), jnp.float32),
            pltpu.VMEM((LOCAL, GROUP, ROWS, WIDTH), jnp.float32),
            pltpu.SemaphoreType.DMA,
            pltpu.SemaphoreType.DMA((LOCAL,)),
            pltpu.SemaphoreType.DMA((LOCAL,)),
        ],
    )(shift_table, movie)
    series = exchange(payload, "frames").reshape(FRAMES * ROWS, WIDTH)
    spatial = spatial_init.reshape(COMP * ROWS, WIDTH)
    stack, spatial_high, spatial_low, mask, gram, picture, upper = call(
        spatial_kernel, "spatial",
        (f32(COMP * ROWS, WIDTH), b16(COMP, TILE), b16(COMP, TILE), f32(COMP, 128), f32(COMP, COMP),
         f32(ROWS, WIDTH), f32(8, 128)),
        [SMEM] + [VMEM] * 3,
        cost=pl.CostEstimate(flops=6 * COMP * COMP * TILE, bytes_accessed=4 << 20, transcendentals=0),
    )(place, spatial, support.T, template.reshape(HEIGHT, WIDTH))
    keep, give, high, low = call(
        cross_kernel, "cross",
        (f32(HALF, PACK), f32(HALF, PACK), b16(FRAMES, TILE), b16(FRAMES, TILE)),
        [VMEM] * 6,
    )(upper, series, picture, spatial_high, spatial_low, gram)

    def spread(kernel, name, values, copies):
        return call(kernel, name, f32(copies, *values.shape[1:]), [VMEM])(values)

    chips = [list(range(core, GROUP, 2)) for core in range(2)]
    part = call(add_kernel, "pair", f32(HALF, PACK), [VMEM] * 2)(keep, swap(give))
    part = exchange(part.reshape(GROUP // 2, LOCAL, PACK), "frames", chips)
    part = exchange(spread(spread_kernel, "spread", part, PLANES), "planes")
    mine = exchange(spread(weigh_kernel, "weigh", part, GROUP // 2), "frames", chips).reshape(HALF, PACK)
    temporal, grad, sums = call(
        step_kernel, "steps",
        (f32(FRAMES, COMP), f32(COMP * ROWS, WIDTH), f32(GROUP, PLANES, 128)),
        [VMEM] * 10,
    )(upper, mine, swap(mine), temporal_init, jnp.asarray(trend_projector()), mask,
      spatial_high, spatial_low, high, low)
    sums = exchange(sums.reshape(GROUP * PLANES, 1, 128), ("frames", "planes"))
    spatial = call(
        final_kernel, "update", f32(COMP * ROWS, WIDTH), [VMEM] * 3, out_specs=HBM,
        scratch_shapes=[
            pltpu.VMEM((COMP * ROWS, WIDTH), jnp.float32), pltpu.SemaphoreType.DMA((BLOCKS,)),
        ],
    )(sums.reshape(GROUP, PLANES, 128), stack, grad)
    return (temporal, spatial.reshape(COMP, 1, TILE))


def solution(mesh):
    placed = (
        P("frames", "planes", None, None),
        P("planes", None, None),
        P("frames", "planes", None),
        P(),
        P(),
        P(None, "planes", "frames"),
    )
    return jax.shard_map(
        body,
        mesh=mesh,
        in_specs=placed,
        out_specs=(P(), P(None, "planes", "frames")),
        check_vma=False,
    )
```
